128 devices in a mesh: grp: 2 (over z_lo), seq: 8 (over z_hi, y), shard: 8 (over x, core).
Axes of the slice: x: 4, y: 4, z: 4 (z_hi: 2, z_lo: 2; z = z_hi * 2 + z_lo), core: 2. Of those that a mesh axis runs over, the one named last changes fastest.
Arguments:
- tokens: bfloat16 [8, 2048, 2048], P('shard', ('grp', 'seq')), may hold values from -6 to 6
- adapter_ids: int32 [8, 5], P('shard'), may hold values from 0 to 7
- norm_gain_attn: bfloat16 [2048], P(('grp', 'seq', 'shard')), may hold values from 0.5 to 1.5
- norm_gain_mlp: bfloat16 [2048], P(('grp', 'seq', 'shard')), may hold values from 0.5 to 1.5
- qkv_weight: bfloat16 [2048, 3072], P(('grp', 'seq', 'shard')), may hold values from -0.4375 to 0.4375
- output_projection_weight: bfloat16 [2048, 2048], P(('grp', 'seq', 'shard')), may hold values from -1 to 1
- gate_up_weight: bfloat16 [2048, 16384], P(('grp', 'seq', 'shard')), may hold values from -0.125 to 0.125
- down_projection_weight: bfloat16 [8192, 2048], P(('grp', 'seq', 'shard')), may hold values from -0.25 to 0.25
- qkv_adapter_in: bfloat16 [2048, 384], P(('grp', 'seq', 'shard')), may hold values from -0.125 to 0.125
- q_adapter_out: bfloat16 [128, 2048], P(('grp', 'seq', 'shard')), may hold values from -0.75 to 0.75
- kv_adapter_out: bfloat16 [128, 1024], P(('grp', 'seq', 'shard')), may hold values from -0.75 to 0.75
- out_adapter_in: bfloat16 [2048, 128], P(('grp', 'seq', 'shard')), may hold values from -0.125 to 0.125
- out_adapter_out: bfloat16 [128, 2048], P(('grp', 'seq', 'shard')), may hold values from -0.75 to 0.75
- gate_up_adapter_in: bfloat16 [2048, 256], P(('grp', 'seq', 'shard')), may hold values from -0.125 to 0.125
- gate_up_adapter_out: bfloat16 [128, 16384], P(('grp', 'seq', 'shard')), may hold values from -0.75 to 0.75
- down_adapter_in: bfloat16 [8192, 128], P(('grp', 'seq', 'shard')), may hold values from -0.0625 to 0.0625
- down_adapter_out: bfloat16 [128, 2048], P(('grp', 'seq', 'shard')), may hold values from -0.75 to 0.75
- cotangent: bfloat16 [8, 2048, 2048], P('shard', ('grp', 'seq')), may hold values from -6 to 6
Outputs:
- output: bfloat16 [8, 2048, 2048], P('shard', ('grp', 'seq'))
- input_grad: bfloat16 [8, 2048, 2048], P('shard', ('grp', 'seq'))
- grad_qkv_adapter_in: float32 [2048, 384], P(('grp', 'seq', 'shard'))
- grad_q_adapter_out: float32 [128, 2048], P(('grp', 'seq', 'shard'))
- grad_kv_adapter_out: float32 [128, 1024], P(('grp', 'seq', 'shard'))
- grad_out_adapter_in: float32 [2048, 128], P(('grp', 'seq', 'shard'))
- grad_out_adapter_out: float32 [128, 2048], P(('grp', 'seq', 'shard'))
- grad_gate_up_adapter_in: float32 [2048, 256], P(('grp', 'seq', 'shard'))
- grad_gate_up_adapter_out: float32 [128, 16384], P(('grp', 'seq', 'shard'))
- grad_down_adapter_in: float32 [8192, 128], P(('grp', 'seq', 'shard'))
- grad_down_adapter_out: float32 [128, 2048], P(('grp', 'seq', 'shard'))
The draws below stay inside these ranges and needn't reach their ends.
All inputs are finite; a program needn't handle non-finite values.
Results may differ from the reference program's by a relative error of at most 0.022.
Values may be sent and summed in bfloat16 or wider, within the bound.
No kernel may reach another device: no remote copies, remote signals or barrier semaphores. Data moves between devices by JAX's collectives and lax.ppermute only.
A program may use at most 384 MiB of HBM per device.

```python
from functools import partial
import jax
import jax.numpy as jnp
from jax import lax

D = 2048
HEADS = 32
KVH = 8
HDIM = 64
FEEDFWD_UNITS = 8192
NAD = 8
RANK = 16
PROMPT = 1024
CONTS = 4
CLEN = 256
GTOK = 2048
GROUPS = 8
KVD = 512
NR = 128


def place_ends(array, stream_key, least, largest):
    longest = array.shape.index(max(array.shape))
    spots = []
    for shift in (0, 1):
        where = [jax.random.randint(jax.random.fold_in(stream_key, axis), (), 0, length) for axis, length in enumerate(array.shape)]
        where[longest] = (where[longest] + shift) % array.shape[longest]
        spots.append(tuple(where))
    return array.at[spots[0]].set(least).at[spots[1]].set(largest)


def shard_levels(key, extent, cuts, least, top_value):
    loudness, own = 1.0, jax.random.fold_in(key, 6)
    for position, blocks in cuts:
        heights = jnp.exp(jax.random.uniform(jax.random.fold_in(own, position), (blocks,), jnp.float32, least / len(cuts), top_value / len(cuts)))
        loudness = loudness * jnp.repeat(heights, extent[position] // blocks).reshape([-1 if axis == position else 1 for axis in range(len(extent))])
    return loudness


def centred(stream_key, extent, spread, limit, pieces=(), kind=jnp.bfloat16):
    level = shard_levels(stream_key, extent, pieces, -0.22, 0.18) if pieces else 1.0
    drawn = jax.random.normal(stream_key, extent, jnp.float32) * spread * level
    return jnp.minimum(jnp.maximum(drawn, -limit), limit).astype(kind)


def setup_inputs(seed: int = 0) -> dict:
    splits = jax.random.split(jax.random.key(seed), 19)
    tokens = centred(splits[0], (GROUPS, GTOK, D), 1.0, 6.0, ((0, 8), (1, 16)))
    adapter_ids = place_ends(jax.random.randint(splits[1], (GROUPS, CONTS + 1), 0, NAD), jax.random.fold_in(splits[1], 1), 0, NAD - 1).astype(jnp.int32)
    norm_gain_attn = jnp.clip(1.0 + 0.1 * jax.random.normal(splits[2], (D,), jnp.float32), 0.5, 1.5).astype(jnp.bfloat16)
    norm_gain_mlp = jnp.clip(1.0 + 0.1 * jax.random.normal(splits[3], (D,), jnp.float32), 0.5, 1.5).astype(jnp.bfloat16)
    qkv_weight = centred(splits[4], (D, D + 2 * KVD), (D // 12) ** -0.5, 0.4375, ((0, 128),))
    output_projection_weight = centred(splits[5], (D, D), (D // 64) ** -0.5, 1.0, ((0, 128),))
    gate_up_weight = centred(splits[6], (D, 2 * FEEDFWD_UNITS), D ** -0.5, 0.125, ((0, 128),))
    down_projection_weight = centred(splits[7], (FEEDFWD_UNITS, D), (FEEDFWD_UNITS // 16) ** -0.5, 0.25, ((0, 128),))
    qkv_adapter_in = centred(splits[8], (D, 3 * NR), D ** -0.5, 0.125, ((0, 128),))
    q_adapter_out = centred(splits[9], (NR, D), (4 * RANK) ** -0.5, 0.75, ((0, 128),))
    kv_adapter_out = centred(splits[10], (NR, 2 * KVD), (4 * RANK) ** -0.5, 0.75, ((0, 128),))
    out_adapter_in = centred(splits[11], (D, NR), D ** -0.5, 0.125, ((0, 128),))
    out_adapter_out = centred(splits[12], (NR, D), (4 * RANK) ** -0.5, 0.75, ((0, 128),))
    gate_up_adapter_in = centred(splits[13], (D, 2 * NR), D ** -0.5, 0.125, ((0, 128),))
    gate_up_adapter_out = centred(splits[14], (NR, 2 * FEEDFWD_UNITS), (4 * RANK) ** -0.5, 0.75, ((0, 128),))
    down_adapter_in = centred(splits[15], (FEEDFWD_UNITS, NR), FEEDFWD_UNITS ** -0.5, 0.0625, ((0, 128),))
    down_adapter_out = centred(splits[16], (NR, D), (4 * RANK) ** -0.5, 0.75, ((0, 128),))
    cotangent = centred(splits[17], (GROUPS, GTOK, D), 1.0, 6.0, ((0, 8), (1, 16)))
    return dict(tokens=tokens, adapter_ids=adapter_ids, norm_gain_attn=norm_gain_attn, norm_gain_mlp=norm_gain_mlp, qkv_weight=qkv_weight, output_projection_weight=output_projection_weight, gate_up_weight=gate_up_weight, down_projection_weight=down_projection_weight, qkv_adapter_in=qkv_adapter_in, q_adapter_out=q_adapter_out, kv_adapter_out=kv_adapter_out, out_adapter_in=out_adapter_in, out_adapter_out=out_adapter_out, gate_up_adapter_in=gate_up_adapter_in, gate_up_adapter_out=gate_up_adapter_out, down_adapter_in=down_adapter_in, down_adapter_out=down_adapter_out, cotangent=cotangent)


@jax.custom_vjp
def lower_precision(v):
    return lax.optimization_barrier(v.astype(jnp.bfloat16)).astype(jnp.float32)

@jax.custom_vjp
def lower_precision_backward(v):
    return v

def low_keep(v):
    return (lower_precision(v), None)

def low_pass(kept, grad):
    return (grad,)

def back_keep(v):
    return (v, None)

def back_low(kept, grad):
    return (lower_precision(grad),)
lower_precision.defvjp(low_keep, low_pass)
lower_precision_backward.defvjp(back_keep, back_low)
EPSILON = 1e-05
ATTN_SCALE = 1.0 / 64.0
SKIP_PATH_SCALE = 0.22
ADAPTER_SCALE = 2.0
ROPE_BASE = 10000000.0
NEG_FILL = -1e+30

def matrix_product(left, right):
    return jnp.dot(left, right, precision=lax.Precision.HIGHEST, preferred_element_type=jnp.float32)

def token_table(token_index):
    offset_after = jnp.maximum(token_index - PROMPT, 0)
    segment_ids = jnp.where(token_index < PROMPT, 0, 1 + offset_after // CLEN).astype(jnp.int32)
    positions = jnp.where(token_index < PROMPT, token_index, PROMPT + offset_after % CLEN).astype(jnp.int32)
    return (segment_ids, positions)

def rope_tables(positions):
    half_dim = HDIM // 2
    frequency = ROPE_BASE ** (-(jnp.arange(half_dim, dtype=jnp.float32) * 2.0) / HDIM)
    angles = positions.astype(jnp.float32)[:, None] * frequency[None, :]
    return (jnp.cos(angles), jnp.sin(angles))

def rotate(value_rows, cosine, sine_rows):
    half_dim = HDIM // 2
    first_half = value_rows[..., :half_dim]
    second_half = value_rows[..., half_dim:]
    cos_part = cosine[:, None, :]
    sin_part = sine_rows[:, None, :]
    return jnp.concatenate([first_half * cos_part - second_half * sin_part, second_half * cos_part + first_half * sin_part], axis=-1)

def rms_normed(value_rows, gain_row):
    return value_rows * lax.rsqrt(lax.optimization_barrier(jnp.mean(value_rows * value_rows, axis=1, keepdims=True)) + EPSILON) * gain_row

def head_block(packed, allowed):
    query_head, key_head, value_head = packed
    scores = lower_precision_backward(jnp.einsum('qrd,kd->rqk', query_head, key_head, precision=lax.Precision.HIGHEST) * ATTN_SCALE)
    scores = jnp.where(allowed[None], scores, NEG_FILL)
    row_max = lax.optimization_barrier(jnp.max(scores, axis=2, keepdims=True))
    exponent = jnp.exp(scores - row_max)
    probs = lower_precision(exponent / lax.optimization_barrier(jnp.sum(exponent, axis=2, keepdims=True)))
    return jnp.einsum('rqk,kd->qrd', probs, value_head, precision=lax.Precision.HIGHEST)

def group_forward(frozen, adapters, group_tokens, ids_row):
    gain_attn, gain_mlp, qkv_weight, output_projection_weight, gate_up_weight, down_projection_weight = frozen
    qkv_in, query_result, key_value_result, out_in, output_projection_result, gu_in, gate_up_result, down_in, down_adapter_result = adapters
    model_width = HEADS * HDIM
    key_value_width = KVH * HDIM
    rank_columns = NAD * RANK
    rep_heads = HEADS // KVH
    token_index = jnp.arange(GTOK, dtype=jnp.int32)
    segment_ids, positions = token_table(token_index)
    cosine, sine_rows = rope_tables(positions)
    chosen = lax.optimization_barrier(jnp.sum(jnp.where(segment_ids[:, None] == jnp.arange(CONTS + 1, dtype=jnp.int32)[None, :], ids_row[None, :], 0), axis=1))
    select_adapter = (jnp.arange(rank_columns, dtype=jnp.int32)[None, :] // RANK == chosen[:, None]).astype(jnp.float32)
    allowed = (token_index[None, :] <= token_index[:, None]) & ((segment_ids[None, :] == 0) | (segment_ids[None, :] == segment_ids[:, None]))
    normed_attn = lower_precision(rms_normed(group_tokens, gain_attn))
    combined_query_key_value = matrix_product(normed_attn, qkv_weight)
    query_key_value_rank_factor = lower_precision(lower_precision_backward(matrix_product(normed_attn, qkv_in))) * jnp.tile(select_adapter, (1, 3))
    query_before_rotation = lower_precision_backward(combined_query_key_value[:, :model_width] + ADAPTER_SCALE * matrix_product(query_key_value_rank_factor[:, :rank_columns], query_result))
    key_before_rotation = lower_precision_backward(combined_query_key_value[:, model_width:model_width + key_value_width] + ADAPTER_SCALE * matrix_product(query_key_value_rank_factor[:, rank_columns:2 * rank_columns], key_value_result[:, :key_value_width]))
    value_rows = lower_precision(lower_precision_backward(combined_query_key_value[:, model_width + key_value_width:] + ADAPTER_SCALE * matrix_product(query_key_value_rank_factor[:, 2 * rank_columns:], key_value_result[:, key_value_width:])))
    queries = lower_precision(rotate(query_before_rotation.reshape(GTOK, HEADS, HDIM), cosine, sine_rows))
    keys = lower_precision(rotate(key_before_rotation.reshape(GTOK, KVH, HDIM), cosine, sine_rows))
    query_heads = queries.reshape(GTOK, KVH, rep_heads, HDIM).transpose(1, 0, 2, 3)
    key_heads = keys.transpose(1, 0, 2)
    value_heads = value_rows.reshape(GTOK, KVH, HDIM).transpose(1, 0, 2)
    attended_heads = lax.map(jax.checkpoint(partial(head_block, allowed=allowed)), (query_heads, key_heads, value_heads))
    attention_output = lower_precision(lower_precision_backward(attended_heads.transpose(1, 0, 2, 3).reshape(GTOK, model_width)))
    output_rank_factor = lower_precision(lower_precision_backward(matrix_product(attention_output, out_in))) * select_adapter
    attention_branch = lower_precision_backward(matrix_product(attention_output, output_projection_weight) + ADAPTER_SCALE * matrix_product(output_rank_factor, output_projection_result))
    hidden_state = group_tokens + SKIP_PATH_SCALE * attention_branch
    normed_mlp = lower_precision(rms_normed(hidden_state, gain_mlp))
    combined_perceptron = matrix_product(normed_mlp, gate_up_weight)
    gate_up_rank_factor = lower_precision(lower_precision_backward(matrix_product(normed_mlp, gu_in))) * jnp.tile(select_adapter, (1, 2))
    gate_activation_value = lower_precision_backward(combined_perceptron[:, :FEEDFWD_UNITS] + ADAPTER_SCALE * matrix_product(gate_up_rank_factor[:, :rank_columns], gate_up_result[:, :FEEDFWD_UNITS]))
    up_projection_value = lower_precision_backward(combined_perceptron[:, FEEDFWD_UNITS:] + ADAPTER_SCALE * matrix_product(gate_up_rank_factor[:, rank_columns:], gate_up_result[:, FEEDFWD_UNITS:]))
    mlp_activation = lower_precision(gate_activation_value * jax.nn.sigmoid(gate_activation_value) * up_projection_value)
    down_rank_factor = lower_precision(lower_precision_backward(matrix_product(mlp_activation, down_in))) * select_adapter
    perceptron_branch = lower_precision_backward(matrix_product(mlp_activation, down_projection_weight) + ADAPTER_SCALE * matrix_product(down_rank_factor, down_adapter_result))
    return hidden_state + SKIP_PATH_SCALE * perceptron_branch

def reference(tokens, adapter_ids, norm_gain_attn, norm_gain_mlp, qkv_weight, output_projection_weight, gate_up_weight, down_projection_weight, qkv_adapter_in, q_adapter_out, kv_adapter_out, out_adapter_in, out_adapter_out, gate_up_adapter_in, gate_up_adapter_out, down_adapter_in, down_adapter_out, cotangent):
    frozen = tuple((item.astype(jnp.float32) for item in (norm_gain_attn, norm_gain_mlp, qkv_weight, output_projection_weight, gate_up_weight, down_projection_weight)))
    adapters = tuple((item.astype(jnp.float32) for item in (qkv_adapter_in, q_adapter_out, kv_adapter_out, out_adapter_in, out_adapter_out, gate_up_adapter_in, gate_up_adapter_out, down_adapter_in, down_adapter_out)))
    layer_input_rows = tokens.astype(jnp.float32)

    def whole_layer(layer_inputs, layer_adapters):

        def one_group(packed):
            return group_forward(frozen, layer_adapters, packed[0], packed[1])
        return lax.map(jax.checkpoint(one_group), (layer_inputs, adapter_ids))
    result, pullback = jax.vjp(whole_layer, layer_input_rows, adapters)
    input_grad, adapter_grads = pullback(cotangent.astype(jnp.float32))
    return (result.astype(jnp.bfloat16), input_grad.astype(jnp.bfloat16), adapter_grads[0], adapter_grads[1], adapter_grads[2], adapter_grads[3], adapter_grads[4], adapter_grads[5], adapter_grads[6], adapter_grads[7], adapter_grads[8])
```

```python
import functools

import jax
import jax.numpy as jnp
from jax import lax
from jax.experimental import pallas as pl
from jax.experimental.pallas import tpu as pltpu
from jax.sharding import Mesh
from jax.sharding import PartitionSpec as P

HEADS = 32
KVH = 8
HDIM = 64
D = HEADS * HDIM
UNITS = 8192
PROMPT = 1024
CLEN = 256
GTOK = 2048
TOK = 128
RANK = 16

EPS = 1e-5
SKIP = 0.22
ROPE_BASE = 10000000.0
NEG = -1e30

F32 = jnp.float32
BF16 = jnp.bfloat16

AXES = ("zl", "zh", "y", "x", "c")
BLOCKS = ("zl", "zh", "y")
NATURAL = ("zh", "zl", "y")
PLANE = ("x", "c")

def mm(a, b):
    return jnp.dot(a, b, preferred_element_type=F32)


def mm_nt(a, b):
    return lax.dot_general(a, b, (((1,), (1,)), ((), ())), preferred_element_type=F32)


def mm_tn(a, b):
    return lax.dot_general(a, b, (((0,), (0,)), ((), ())), preferred_element_type=F32)


def swap_mid(v, axis=-1):
    axis = axis % v.ndim
    n = v.shape[axis] // 4
    q = [lax.slice_in_dim(v, k * n, (k + 1) * n, axis=axis) for k in (0, 2, 1, 3)]
    return jnp.concatenate(q, axis=axis)


def a2a(v, axes):
    return lax.all_to_all(v, axes, 0, 0, tiled=True)


def other_core(v):
    return lax.ppermute(v, "c", [(0, 1), (1, 0)])


def along_x(v, k):
    return lax.ppermute(v, "x", [(i, (i + k) % 4) for i in range(4)])


MIB = 1024 * 1024


def nbytes(arrays):
    return sum(a.size * a.dtype.itemsize for a in arrays)


def job(g, j):
    return (j // 2) * 4 + g * 2 + j % 2


def far_of(one, three):
    half = one.shape[0] // 2
    return jnp.concatenate([along_x(one[:half], 1), along_x(three[half:], 3)])


def from_x(v):
    one, three = along_x(v, 1), along_x(v, 3)
    return one, three, far_of(one, three)


def call(kernel, outs, args, scratch=(), specs=None, flops=0, vmem=24):
    if specs is None:
        specs = [None] * len(args)
    ins = [pl.BlockSpec(memory_space=pltpu.VMEM) if s is None else s for s in specs]
    return pl.pallas_call(
        kernel,
        grid=(1,),
        out_shape=outs,
        in_specs=ins,
        out_specs=[pl.BlockSpec(memory_space=pltpu.VMEM)] * len(outs),
        scratch_shapes=list(scratch),
        compiler_params=pltpu.CompilerParams(vmem_limit_bytes=vmem * MIB),
        cost_estimate=pl.CostEstimate(
            flops=flops, bytes_accessed=nbytes(args) + nbytes(outs), transcendentals=0
        ),
    )(*args)


def tiled_call(kernel, outs, args, specs, out_specs, scratch=(), flops=0, steps=4, vmem=32):
    size = nbytes(outs) + 2 * flops // 1024
    return pl.pallas_call(
        kernel,
        grid=(steps,),
        out_shape=outs,
        in_specs=specs,
        out_specs=out_specs,
        scratch_shapes=list(scratch),
        compiler_params=pltpu.CompilerParams(vmem_limit_bytes=vmem * MIB),
        cost_estimate=pl.CostEstimate(flops=flops, bytes_accessed=size, transcendentals=0),
    )(*args)


def shape(*dims, dtype=F32):
    return jax.ShapeDtypeStruct(dims, dtype)


def block(rows, cols, index):
    return pl.BlockSpec((rows, cols), lambda i: (0, index), pipeline_mode=pl.Buffered(1))


def whole_spec(rows, cols):
    return pl.BlockSpec((rows, cols), lambda i: (0, 0))


def after(v, *others):
    return lax.optimization_barrier((v, others))[0]


def segment_of(block_index):
    return jnp.where(block_index < 8, 0, 1 + (block_index - 8) // 2)


SMEM = pl.BlockSpec(memory_space=pltpu.SMEM)


def rope(t, cos, sin):
    lane = lax.broadcasted_iota(jnp.int32, t.shape, 1) % HDIM
    partner = jnp.where(lane < HDIM // 2, pltpu.roll(t, 96, 1), pltpu.roll(t, 32, 1))
    return t * cos + partner * sin


def assemble(x, pieces, whole):
    for piece, ahead in zip(pieces, (0, 3, 1, 2)):
        at = lax.rem(x + ahead, 4) * 32

        def place(i, _, piece=piece, at=at):
            to = pl.multiple_of(i * 128 + at, 32)
            whole[pl.ds(to, 32), :] = piece[pl.ds(pl.multiple_of(i * 32, 32), 32), :]
            return 0

        lax.fori_loop(0, 16, place, 0)


def gain_row(g, first):
    lane = lax.broadcasted_iota(jnp.int32, (128, 128), 1)
    row = lax.broadcasted_iota(jnp.int32, (128, 128), 0)
    tiled = mm(g.astype(BF16), (row == first + lane % 16).astype(BF16))
    tiled = jnp.where(lane // 16 == row % 8, tiled, 0.0).astype(BF16)
    to_row = lax.broadcasted_iota(jnp.int32, (16, 128), 1) // 8
    to_row = (to_row == lax.broadcasted_iota(jnp.int32, (16, 128), 0)).astype(BF16)
    rows = mm(to_row, tiled)
    return jnp.concatenate([rows[k : k + 1] for k in range(16)], axis=1)


def only_keys(kv):
    lane = lax.broadcasted_iota(jnp.int32, kv.shape, 1) % 128
    return jnp.where(lane < HDIM, kv, 0.0).astype(BF16), jnp.where(lane < HDIM, 0.0, kv).astype(BF16)


def qkv_kernel(
    place, x, e, pick, cq, sq, ckv, skv, send, normed, small, gain, gain_mlp, n, s_all, wide
):
    core = place[1]
    wide[...] = e[:, 768:896].astype(F32)
    q_out = jnp.concatenate([wide[pl.ds(t, 128, stride=16), :] for t in range(2)], axis=1)
    q_out = q_out.astype(BF16)
    k_out, v_out = only_keys(wide[pl.ds(2, 128, stride=16), :])
    gain[...] = gain_row(wide[pl.ds(3, 128, stride=16), :], 0)
    gain_mlp[...] = gain_row(wide[pl.ds(3, 128, stride=16), :], 16)
    for k in range(4):
        rows = slice(2 * k * TOK, (2 * k + 2) * TOK)
        v = x[rows, :].astype(F32)
        r = lax.rsqrt(jnp.mean(v * v, axis=1, keepdims=True) + EPS)
        n[rows, :] = (v * r * gain[...]).astype(BF16)
        s = mm(n[rows, :], e[:, 384:768]).astype(BF16)
        s = jnp.concatenate(
            [s[:TOK] * pick[2 * k : 2 * k + 1, :], s[TOK:] * pick[2 * k + 1 : 2 * k + 2, :]], axis=0
        )
        s_all[rows, :] = s
        q = mm(n[rows, :], e[:, :256]) + 2.0 * mm(s[:, :128], q_out)
        kv = mm(n[rows, :], e[:, 256:384]) + 2.0 * (
            mm(s[:, 128:256], k_out) + mm(s[:, 256:], v_out)
        )
        for o in range(2):
            here = slice(o * TOK, (o + 1) * TOK)
            t = rope(kv[here], ckv[...], skv[...]).astype(BF16)
            at = k * 4 + 2 * lax.rem(core + o, 2)
            for j in range(2):
                p = rope(q[here, j * 128 : (j + 1) * 128], cq[...], sq[...]).astype(BF16)
                send[at + j, :, 0:128] = p
                send[at + j, :, 128:256] = t
    own = pl.multiple_of((2 * place[0] + core) * TOK, TOK)
    other = pl.multiple_of((2 * place[0] + 1 - core) * TOK, TOK)
    normed[...] = n[pl.ds(own, TOK), :]
    small[:TOK, :] = s_all[pl.ds(own, TOK), :]
    small[TOK:, :] = s_all[pl.ds(other, TOK), :]


def heads_of(ref, rows, scale=None):
    t = ref[rows, :128]
    both = jnp.concatenate([t[:, :HDIM], t[:, HDIM:]], axis=0)
    return both if scale is None else both * jnp.asarray(scale, BF16)


def allowed_in_block():
    key = lax.broadcasted_iota(jnp.int32, (CLEN, 2 * CLEN), 0)
    query = lax.broadcasted_iota(jnp.int32, (CLEN, 2 * CLEN), 1) % CLEN
    return key <= query


def attend_kernel(z, out, stat):
    allowed = allowed_in_block()
    for i in range(GTOK // CLEN):
        rows = slice(i * CLEN, (i + 1) * CLEN)
        full = min(i, PROMPT // CLEN) * CLEN
        q = heads_of(z, rows, 1.0 / 64.0)
        sd = jnp.where(allowed, mm_nt(z[rows, 128:192], q), NEG)
        top = jnp.max(sd, axis=0, keepdims=True)
        if full:
            sf = mm_nt(z[0:full, 128:192], q)
            top = jnp.maximum(top, jnp.max(sf, axis=0, keepdims=True))
        pd = jnp.exp(sd - top)
        total = jnp.sum(pd, axis=0, keepdims=True)
        o = mm_tn(z[rows, 192:256], pd.astype(BF16))
        if full:
            pf = jnp.exp(sf - top)
            total = total + jnp.sum(pf, axis=0, keepdims=True)
            o = o + mm_tn(z[0:full, 192:256], pf.astype(BF16))
        o = o / total
        stat[i : i + 1, :] = top + jnp.log(total)
        both = jnp.concatenate([o[:, :CLEN], o[:, CLEN:]], axis=0)
        out[rows, :] = both.T.astype(BF16)


def attend_back_kernel(z, d_out, stat, dz, dk, dv):
    allowed = allowed_in_block()
    dk[...] = jnp.zeros_like(dk)
    dv[...] = jnp.zeros_like(dv)
    for i in range(GTOK // CLEN):
        rows = slice(i * CLEN, (i + 1) * CLEN)
        full = min(i, PROMPT // CLEN) * CLEN
        q = heads_of(z, rows, 1.0 / 64.0)
        do = heads_of(d_out, rows)
        lse = stat[i : i + 1, :]
        kd = z[rows, 128:192]
        pd = jnp.exp(jnp.where(allowed, mm_nt(kd, q), NEG) - lse)
        dpd = mm_nt(z[rows, 192:256], do)
        inner = jnp.sum(pd * dpd, axis=0, keepdims=True)
        if full:
            kf = z[0:full, 128:192]
            pf = jnp.exp(mm_nt(kf, q) - lse)
            dpf = mm_nt(z[0:full, 192:256], do)
            inner = inner + jnp.sum(pf * dpf, axis=0, keepdims=True)
        dsd = (pd * (dpd - inner)).astype(BF16)
        dq = mm_tn(kd, dsd)
        dk[rows, :] += mm(dsd, q)
        dv[rows, :] += mm(pd.astype(BF16), do)
        if full:
            dsf = (pf * (dpf - inner)).astype(BF16)
            dq = dq + mm_tn(kf, dsf)
            dk[0:full, :] += mm(dsf, q)
            dv[0:full, :] += mm(pf.astype(BF16), do)
        dq = dq * (1.0 / 64.0)
        both = jnp.concatenate([dq[:, :CLEN], dq[:, CLEN:]], axis=0)
        dz[rows, 0:128] = both.T.astype(BF16)
    dz[:, 128:256] = jnp.concatenate([dk[...], dv[...]], axis=1).astype(BF16)


def project_kernel(
    place, mine, theirs, e0, e1, e2, e3, pick, part, small, attended, whole, a_out, att, wide
):
    assemble(place[0], (e0, e1, e2, e3), whole)
    wide[...] = whole[:, 1152:1280].astype(F32)
    for t in range(16):
        a_out[:, t * 128 : (t + 1) * 128] = wide[pl.ds(t, 128, stride=16), :].astype(BF16)
    c = place[1]
    here = pl.multiple_of(c * 1024, 1024)
    there = pl.multiple_of((1 - c) * 1024, 1024)
    for g in range(2):
        rows = slice(g * TOK, (g + 1) * TOK)
        for j in range(8):
            cols = slice(j * 128, (j + 1) * 128)
            att[0, rows, cols] = mine[job(g, j)]
            att[1, rows, cols] = theirs[job(1 - g, j)]
    m, t = att[0], att[1]
    attended[:, pl.ds(here, 1024)] = m[:TOK]
    attended[:, pl.ds(there, 1024)] = t[:TOK]
    s = mm(m, whole[pl.ds(here, 1024), 1024:1152]) + mm(t, whole[pl.ds(there, 1024), 1024:1152])
    s = s.astype(BF16)
    s = jnp.concatenate([s[:TOK] * pick[0:1, :128], s[TOK:] * pick[1:2, :128]], axis=0)
    small[...] = s
    part[...] = (
        mm(m, whole[pl.ds(here, 1024), :1024])
        + mm(t, whole[pl.ds(there, 1024), :1024])
        + 2.0 * mm(s, a_out[:, pl.ds(here, 1024)])
    )


def hidden_kernel(place, x, mine, theirs, gain, hidden, normed):
    c = place[1]
    here = pl.multiple_of(c * 1024, 1024)
    there = pl.multiple_of((1 - c) * 1024, 1024)
    hidden[:, pl.ds(here, 1024)] = SKIP * mine[...]
    hidden[:, pl.ds(there, 1024)] = SKIP * theirs[...]
    h = x[...].astype(F32) + hidden[...]
    hidden[...] = h
    r = lax.rsqrt(jnp.mean(h * h, axis=1, keepdims=True) + EPS)
    normed[...] = (h * r * gain[...]).astype(BF16)


def unpack_kernel(outs, gu_out, down_out, wide):
    for k in range(3):
        wide[...] = outs[:, k * 128 : (k + 1) * 128].astype(F32)
        for t in range(16):
            at = (3 * t + k) * 128
            part = wide[pl.ds(t, 128, stride=16), :].astype(BF16)
            if at < 4096:
                gu_out[:, at : at + 128] = part
            else:
                down_out[:, at - 4096 : at - 3968] = part


def turn_kernel(cot, dm, turned):
    d = (SKIP * cot[...].astype(F32)).astype(BF16)
    dm[...] = d
    turned[...] = d.T


def d_act_kernel(dm, turned, a_out, a_in, pick, w, d_act, small):
    @pl.when(pl.program_id(0) == 0)
    def _():
        s = 2.0 * mm_nt(dm[...], a_out[...]) * pick[...].astype(F32)
        small[...] = s.astype(BF16)

    d_act[...] = mm(w[...], turned[...]).T + mm_nt(small[...], a_in[...])


def feed_kernel(
    n, d_act, pick, w_gate, w_up, o_gate, o_up, a_in, a_down, g_gate0, g_up0,
    act, back, g_gate, g_up, total, small,
):
    step = pl.program_id(0)

    @pl.when(step == 0)
    def _():
        s = mm(n[...], a_in[...]).astype(BF16)
        p = pick[...]
        small[...] = s * jnp.concatenate([p, p], axis=1)
        total[...] = jnp.zeros_like(total)

    x = n[...]
    gate = mm(x, w_gate[...]) + 2.0 * mm(small[:, :128], o_gate[...])
    up = mm(x, w_up[...]) + 2.0 * mm(small[:, 128:], o_up[...])
    sg = 1.0 / (1.0 + jnp.exp(-gate))
    gs = gate * sg
    act[...] = (gs * up).astype(BF16)
    da = d_act[...]
    dg = (da * up * (sg + gs * (1.0 - sg))).astype(BF16)
    du = (da * gs).astype(BF16)
    total[:D, :] += mm_nt(w_gate[...], dg) + mm_nt(w_up[...], du)
    total[D : D + 128, :] += mm_nt(o_gate[...], dg)
    total[D + 128 : D + 256, :] += mm_nt(o_up[...], du)
    total[D + 256 :, :] += mm_nt(a_down[...].T, act[...])
    for t in range(4):
        cols = slice(t * 128, (t + 1) * 128)
        g = mm_tn(small[:, :128], dg[:, cols]).reshape(16, 8, 128)
        g_gate[:, t] = g_gate0[:, t] + g
        g = mm_tn(small[:, 128:], du[:, cols]).reshape(16, 8, 128)
        g_up[:, t] = g_up0[:, t] + g

    @pl.when(step == pl.num_programs(0) - 1)
    def _():
        back[...] = total[...].T.astype(BF16)


def down_kernel(act_a, act_b, d_small, w, out, g_in, total):
    step = pl.program_id(0)

    @pl.when(step == 0)
    def _():
        total[...] = jnp.zeros_like(total)

    for k, act in enumerate((act_a, act_b)):
        rows = slice(k * 256, (k + 1) * 256)
        total[rows, :] += mm(act[...], w[...])
    g = mm_tn(act_a[...], d_small[:256]) + mm_tn(act_b[...], d_small[256:])
    g_in[...] = g.astype(BF16)

    @pl.when(step == pl.num_programs(0) - 1)
    def _():
        out[...] = total[...].astype(BF16)


def output_kernel(hidden, p0, p1, p2, p3, a_out, small, out):
    total = p0[...].astype(F32) + p1[...].astype(F32) + p2[...].astype(F32) + p3[...].astype(F32)
    out[...] = (hidden[...] + SKIP * (total + 2.0 * mm(small[...], a_out[...]))).astype(BF16)


def rms_back(v, gain, e):
    r = lax.rsqrt(jnp.mean(v * v, axis=1, keepdims=True) + EPS)
    we = gain * e
    return r * we - v * (r * r * r) * jnp.mean(v * we, axis=1, keepdims=True)


def d_hidden_kernel(
    hidden, cot, gain, p0, p1, p2, p3, a_in, pick, d_hidden, d_attn, small, small_down
):
    total = p0[...].astype(F32) + p1[...].astype(F32) + p2[...].astype(F32) + p3[...].astype(F32)
    s = (2.0 * total[:, D : D + 256] * pick[0:1, :256]).astype(BF16)
    small[...] = s
    small_down[...] = (total[:, D + 256 :] * pick[0:1, :128]).astype(BF16)
    e = total[:, :D] + mm_nt(s, a_in[...])
    d = cot[...].astype(F32) + rms_back(hidden[...], gain[...], e)
    d_hidden[...] = d
    d_attn[...] = (SKIP * d).astype(BF16)


def project_back_kernel(place, own, other, w, a_in, a_out, pick, mine, theirs, small, halves):
    c = place[1]
    here = pl.multiple_of(c * 1024, 1024)
    there = pl.multiple_of((1 - c) * 1024, 1024)
    full = jnp.concatenate([own[...], other[...]], axis=0)
    s = 2.0 * mm_nt(full, a_out[...])
    s = jnp.concatenate([s[:TOK] * pick[0:1, :128], s[TOK:] * pick[1:2, :128]], axis=0)
    s = s.astype(BF16)
    small[...] = s
    half = jnp.concatenate([own[:, pl.ds(here, 1024)], other[:, pl.ds(here, 1024)]], axis=0)
    halves[...] = half
    theirs[...] = mm_nt(half, w[pl.ds(there, 1024), :]).astype(BF16)
    mine[...] = mm_nt(half, w[pl.ds(here, 1024), :]) + mm_nt(s, a_in[pl.ds(here, 1024), :])


def pack_kernel(mine, theirs, send):
    for g in range(2):
        rows = slice(g * TOK, (g + 1) * TOK)
        swapped = slice((1 - g) * TOK, (2 - g) * TOK)
        for j in range(8):
            cols = slice(j * 128, (j + 1) * 128)
            send[job(g, j)] = (mine[rows, cols] + theirs[swapped, cols].astype(F32)).astype(BF16)


def early_grads_kernel(
    gu, g_down_in, d_small_gu, normed, small_down, cot, d_small_o, attended, small_o, halves, fold,
    out, lines,
):
    f = mm(d_small_gu[...], fold[:256, :]).astype(BF16)[:, :HDIM]
    g = mm_tn(f, normed[...])
    f = mm(d_small_o[:TOK], fold[256:384, :]).astype(BF16)[:, :HDIM]
    g = g + mm_tn(f, attended[...])
    dm = (SKIP * cot[...].astype(F32)).astype(BF16)
    g_down = 2.0 * mm_tn(small_down[...], dm)
    g_o = 2.0 * mm_tn(small_o[...], halves[...])
    for k in range(16):
        lines[k, 128:192, :] = g[:, k * 128 : (k + 1) * 128]
        rows = slice(k * 8, (k + 1) * 8)
        for t in range(16):
            lines[k, 192 + t * 8 : 200 + t * 8, :] = g_down[rows, t * 128 : (t + 1) * 128]
        for t in range(8):
            lines[k, 320 + t * 8 : 328 + t * 8, :] = g_o[rows, t * 128 : (t + 1) * 128]
        out[k, :128, :] = g_down_in[k * 128 : (k + 1) * 128, :]
        out[k, 128:384, :] = lines[k, 128:, :].astype(BF16)
        out[k, 384:, :] = gu[k]


def sums_kernel(slot, early, plane, g_down_in, first, total):
    first[...] = jnp.zeros_like(first)
    total[...] = early[0, 384:, :].astype(F32)
    for k in range(1, 16):
        total[...] += early[k, 384:, :].astype(F32)
    for r in range(8):
        plane[r, 0:32, :] = total[pl.ds(r, 32, stride=8), :]
    d = early[0, :128, :].astype(F32)
    o = early[0, 192:384, :].astype(F32)
    for k in range(16):
        at = pl.multiple_of(slot[k] * HDIM, HDIM)
        first[pl.ds(at, HDIM), :] += early[k, 128:192, :].astype(F32)
        if k:
            d = d + early[k, :128, :].astype(F32)
            o = o + early[k, 192:384, :].astype(F32)
    g_down_in[...] = d
    total[:192, :] = o
    turned = first[...].T
    for r in range(8):
        for k in range(4):
            part = turned[r * 16 : (r + 1) * 16, k * 128 : (k + 1) * 128]
            plane[r, 32 + k * 16 : 48 + k * 16, :] = part
        plane[r, 96:120, :] = total[pl.ds(r, 24, stride=8), :]


def unpack_qkv_kernel(outs, q_out, k_out, v_out, wide):
    wide[...] = outs[...].astype(F32)
    q = [wide[pl.ds(t, 128, stride=16), :] for t in range(8)]
    q_out[...] = jnp.concatenate(q, axis=1).astype(BF16)
    kv = [wide[pl.ds(8 + t, 128, stride=16), :] for t in range(4)]
    k_out[...], v_out[...] = only_keys(jnp.concatenate(kv, axis=1))


def qkv_back_kernel(
    parts, q_out, k_out, v_out, cq, sq, ckv, skv, d_joint, mine_small, their_small
):
    for g in range(2):
        rows = slice(g * TOK, (g + 1) * TOK)
        for j in range(8):
            t = parts[job(g, j), :, 0:128].astype(F32)
            d_joint[rows, j * 128 : (j + 1) * 128] = rope(t, cq[...], -sq[...]).astype(BF16)
        for j in range(4):
            t = parts[job(g, 2 * j), :, 128:256].astype(F32)
            t = t + parts[job(g, 2 * j + 1), :, 128:256].astype(F32)
            d_joint[rows, 1024 + j * 128 : 1024 + (j + 1) * 128] = rope(
                t, ckv[...], -skv[...]
            ).astype(BF16)
    dq, dkv = d_joint[:, :1024], d_joint[:, 1024:]
    small = 2.0 * jnp.concatenate(
        [mm_nt(dq, q_out[...]), mm_nt(dkv, k_out[...]), mm_nt(dkv, v_out[...])], axis=1
    )
    mine_small[...] = small[:TOK]
    their_small[...] = small[TOK:].astype(BF16)


def late_grads_kernel(
    mine_small, their_small, pick, normed, small_qkv, d_joint, fold, small, out, g
):
    s = ((mine_small[...] + their_small[...].astype(F32)) * pick[0:1, :]).astype(BF16)
    small[...] = s
    f = mm(s, fold[...]).astype(BF16)
    out[:, :128] = mm_tn(normed[...], f).astype(BF16)
    gq = 2.0 * mm_tn(small_qkv[:, :128], d_joint[:, :1024])
    gk = mm_tn(small_qkv[:, 128:256], d_joint[:, 1024:])
    gv = mm_tn(small_qkv[:, 256:], d_joint[:, 1024:])
    lane = lax.broadcasted_iota(jnp.int32, gk.shape, 1) % 128
    gkv = 2.0 * jnp.where(lane < HDIM, gk, gv)
    for t in range(8):
        g[pl.ds(t, 128, stride=16), :] = gq[:, t * 128 : (t + 1) * 128]
    for t in range(4):
        g[pl.ds(8 + t, 128, stride=16), :] = gkv[:, t * 128 : (t + 1) * 128]
        g[pl.ds(12 + t, 128, stride=16), :] = jnp.zeros((128, 128), F32)
    out[:, 128:] = g[...].astype(BF16)


def late_sums_kernel(slot, late, first, second):
    first[...] = jnp.zeros_like(first)
    second[...] = jnp.zeros_like(second)

    def add(k, _):
        for core in range(2):
            v = late[2 * k + core].astype(F32)
            at = slot[2 * k + core]
            first[at] += v[:, :128]
            second[core] += v[:, 128:]
        return 0

    lax.fori_loop(0, 64, add, 0)


def d_normed_kernel(d_joint, w, mine, theirs):
    dn = mm_nt(d_joint[...], w[...])
    mine[...] = dn[:TOK]
    theirs[...] = dn[TOK:].astype(BF16)


def last_kernel(x, d_hidden, gain, mine, theirs, small, a, grad):
    dn = mine[...] + theirs[...].astype(F32) + mm_nt(small[...], a[...])
    v = x[...].astype(F32)
    grad[...] = (d_hidden[...] + rms_back(v, gain[...], dn)).astype(BF16)


def local(
    tokens,
    adapter_ids,
    norm_gain_attn,
    norm_gain_mlp,
    qkv_weight,
    output_projection_weight,
    gate_up_weight,
    down_projection_weight,
    qkv_adapter_in,
    q_adapter_out,
    kv_adapter_out,
    out_adapter_in,
    out_adapter_out,
    gate_up_adapter_in,
    gate_up_adapter_out,
    down_adapter_in,
    down_adapter_out,
    cotangent,
):
    c = lax.axis_index("c")
    x = lax.axis_index("x")
    b = lax.axis_index(BLOCKS)
    place = jnp.stack([x, c]).astype(jnp.int32)

    x_own = swap_mid(tokens[0])
    cot_own = swap_mid(cotangent[0])
    x_plane = lax.all_gather(x_own, PLANE, axis=0, tiled=True)

    q_w = swap_mid(qkv_weight[:, :D])
    k_w = swap_mid(qkv_weight[:, D : D + 512]).reshape(16, 8, 1, HDIM)
    v_w = swap_mid(qkv_weight[:, D + 512 :]).reshape(16, 8, 1, HDIM)
    kv_w = jnp.concatenate([k_w, v_w], axis=2).reshape(16, 1024)
    a_in = swap_mid(qkv_adapter_in.reshape(16, 3, 128)).reshape(16, 384)
    qo = swap_mid(q_adapter_out)
    ko = swap_mid(kv_adapter_out[:, :512]).reshape(8, 1, HDIM)
    vo = swap_mid(kv_adapter_out[:, 512:]).reshape(8, 1, HDIM)
    kvo = jnp.concatenate([ko, vo], axis=1).reshape(1, 1024)
    ids = adapter_ids[0]
    extra = jnp.concatenate([norm_gain_attn, norm_gain_mlp, ids.astype(BF16), jnp.zeros(91, BF16)])
    outs = jnp.concatenate(
        [
            qo.reshape(8, 2, 128),
            kvo.reshape(8, 1, 128),
            jnp.broadcast_to(extra, (8, 1, 128)),
            jnp.zeros((8, 12, 128), BF16),
        ],
        axis=1,
    )
    payload = jnp.concatenate(
        [
            q_w.reshape(16, 8, 256).transpose(1, 0, 2),
            kv_w.reshape(16, 8, 128).transpose(1, 0, 2),
            jnp.broadcast_to(a_in, (8, 16, 384)),
            outs,
        ],
        axis=2,
    )
    heads = payload.reshape(2, 4, 16, 896).transpose(1, 0, 2, 3).reshape(8, 16, 896)
    heads = a2a(heads, PLANE)
    ids_all = heads[:, 3, 800:805].astype(F32)
    heads = jnp.broadcast_to(heads.reshape(1, 128, 896), (16, 128, 896))
    heads = a2a(heads, NATURAL).reshape(D, 896)

    o_w = swap_mid(output_projection_weight).reshape(16, 2, 1024)
    o_out = swap_mid(out_adapter_out).reshape(16, 128)
    payload = jnp.concatenate(
        [
            o_w.transpose(1, 0, 2),
            jnp.broadcast_to(swap_mid(out_adapter_in), (2, 16, 128)),
            jnp.broadcast_to(o_out, (2, 16, 128)),
        ],
        axis=2,
    )

    def chip_rows(v):
        keep = lax.dynamic_index_in_dim(v, c, 0, keepdims=False)
        take = other_core(lax.dynamic_index_in_dim(v, 1 - c, 0, keepdims=False))
        return jnp.where(c == 0, jnp.concatenate([keep, take]), jnp.concatenate([take, keep]))

    chip = chip_rows(payload)
    o_mine = lax.all_gather(after(chip, x_plane), NATURAL, axis=0, tiled=True)
    o_set = [o_mine, *from_x(o_mine)]

    gu = gate_up_weight.reshape(16, 2, 2, 2, 4, 4, 128).transpose(5, 0, 1, 3, 2, 4, 6)
    gu = gu.reshape(4, 16, 4096)
    guo = gate_up_adapter_out.reshape(2, 2, 2, 4, 4, 128).transpose(4, 0, 2, 1, 3, 5)
    guo = guo.reshape(4, 4096)
    outs = jnp.concatenate([guo, jnp.broadcast_to(swap_mid(down_adapter_out), (4, D))], axis=1)
    gu_in = swap_mid(gate_up_adapter_in.reshape(16, 2, 128)).reshape(16, 256)
    to_x = jnp.concatenate(
        [
            gu,
            jnp.broadcast_to(gu_in, (4, 16, 256)),
            outs.reshape(4, 16, 384),
        ],
        axis=2,
    )

    def for_chip(k):
        return lax.dynamic_index_in_dim(to_x, (x + k) % 4, 0, keepdims=False)

    by_chip = [for_chip(0)] + [along_x(for_chip(k), k) for k in (1, 2, 3)]
    by_chip = jnp.stack(by_chip)

    def of_pair(core):
        two = [
            lax.dynamic_index_in_dim(by_chip, (x - 2 * core - j) % 4, 0, keepdims=False)
            for j in range(2)
        ]
        return jnp.stack(two)

    keep = of_pair(c)
    take = other_core(of_pair(1 - c))
    rows = jnp.where(c == 0, jnp.stack([keep, take], 1), jnp.stack([take, keep], 1))
    plane = rows.reshape(64, 4736)
    down_w = swap_mid(down_projection_weight)
    down_in = swap_mid(down_adapter_in)
    plane = jnp.concatenate(
        [plane[:, :4096], down_w, plane[:, 4096:4352], down_in, plane[:, 4352:]], axis=1
    )

    mlp_set = lax.all_gather(after(plane, heads), NATURAL + ("c",), axis=0, tiled=True)

    segment = segment_of(b)
    start = jnp.where(b < 8, b * TOK, PROMPT + ((b - 8) % 2) * TOK)
    positions = start + jnp.arange(TOK, dtype=jnp.int32)
    frequency = ROPE_BASE ** (-(jnp.arange(HDIM // 2, dtype=F32) * 2.0) / HDIM)
    angles = positions.astype(F32)[:, None] * frequency[None, :]
    cos, sin = jnp.cos(angles), jnp.sin(angles)
    one, zero = jnp.ones((TOK, HDIM), F32), jnp.zeros((TOK, HDIM), F32)
    cq = jnp.concatenate([cos] * 4, axis=1)
    sq = jnp.concatenate([-sin, sin, -sin, sin], axis=1)
    ckv = jnp.concatenate([cos, cos, one], axis=1)
    skv = jnp.concatenate([-sin, sin, zero], axis=1)

    col = jnp.arange(128)
    col_adapter = ((col >> 5) & 1) * 4 + ((col >> 6) & 1) * 2 + ((col >> 4) & 1)
    here = (jnp.arange(5) == segment).astype(F32)

    def picks(adapters):
        a = jnp.sum(adapters.astype(F32) * here)
        return (col_adapter.astype(F32) == a).astype(BF16)

    def picks_at(ahead, core):
        row = 2 * ((x + ahead) % 4) + core
        return picks(lax.dynamic_index_in_dim(ids_all, row, 0, keepdims=False))

    pick = jnp.stack([jnp.tile(picks(ids_all[k]), 3) for k in range(8)])
    pick_all = jnp.concatenate([pick, jnp.zeros((8, 384), BF16)], axis=0)
    pick = [lax.dynamic_slice_in_dim(pick, 2 * x + core, 1) for core in (c, 1 - c)]
    pick = jnp.concatenate([*pick, jnp.zeros((14, 384), BF16)], axis=0)
    pick_f = pick.astype(F32)

    send, normed_attn, small_qkv, gain_attn, gain_mlp = call(
        qkv_kernel,
        [
            shape(16, TOK, 256, dtype=BF16),
            shape(TOK, D, dtype=BF16),
            shape(256, 384, dtype=BF16),
            shape(1, D),
            shape(1, D),
        ],
        [place, after(x_plane, plane), heads, pick_all, cq, sq, ckv, skv],
        scratch=[
            pltpu.VMEM((1024, D), BF16),
            pltpu.VMEM((1024, 384), BF16),
            pltpu.VMEM((D, 128), F32),
        ],
        specs=[SMEM] + [None] * 7,
        flops=2 * 1024 * D * 768,
        vmem=40,
    )
    z = a2a(a2a(send, "x"), BLOCKS).reshape(GTOK, 256)
    cot = [cot_own, *from_x(after(cot_own, o_set))]
    cot = jnp.concatenate([cot[1], cot[2], cot[0], cot[3]])

    t2 = jnp.concatenate(
        [
            q_w.reshape(16, 2, 1024).transpose(1, 0, 2),
            kv_w.reshape(16, 2, 512).transpose(1, 0, 2),
            jnp.concatenate(
                [qo.reshape(2, 8, 128), kvo.reshape(2, 4, 128), jnp.zeros((2, 4, 128), BF16)], axis=1
            ),
        ],
        axis=2,
    )
    t2 = chip_rows(t2)
    rel = jnp.stack([t2] + [along_x(t2, k) for k in (1, 2, 3)])
    rel = [lax.dynamic_index_in_dim(rel, (x - k) % 4, 0, keepdims=False) for k in range(4)]
    t2 = jnp.concatenate(rel)

    attended, stat = call(
        attend_kernel,
        [shape(GTOK, 128, dtype=BF16), shape(8, 512)],
        [after(z, o_set[:3])],
        flops=2 * 2 * 2 * 30 * CLEN * CLEN * HDIM * 4,
        vmem=20,
    )
    mine = a2a(after(attended, t2, o_set).reshape(16, TOK, 128), BLOCKS)
    theirs = other_core(mine)
    part, small_o, attended, o_whole, out_out = call(
        project_kernel,
        [
            shape(256, 1024),
            shape(256, 128, dtype=BF16),
            shape(TOK, D, dtype=BF16),
            shape(D, 1280, dtype=BF16),
            shape(128, D, dtype=BF16),
        ],
        [place, mine, after(theirs, cot), *o_set, pick],
        scratch=[pltpu.VMEM((2, 256, 1024), BF16), pltpu.VMEM((D, 128), F32)],
        specs=[SMEM] + [None] * 7,
        flops=2 * 256 * D * 1024,
        vmem=24,
    )
    w_spec = block(D, 1536, 0)
    o_spec = block(D, 1024, 0)
    oa_spec = block(D, 128, 8)

    device = jnp.arange(128)
    device_segment = segment_of(((device >> 5) & 1) * 8 + (device >> 6) * 4 + ((device >> 3) & 3))
    device_segment = (device_segment[:, None] == jnp.arange(5)).astype(F32)
    device_ids = jnp.broadcast_to(ids_all[None], (16, 8, 5)).reshape(128, 5)
    device_adapter = jnp.sum(device_ids * device_segment, axis=1)
    natural = device_adapter.astype(jnp.int32)
    device_slot = (natural >> 1 & 1) * 4 + (natural >> 2) * 2 + (natural & 1)
    source_slot = lax.dynamic_slice_in_dim(
        device_slot.reshape(16, 8).T.reshape(128), (2 * x + c) * 16, 16
    )
    lane = jnp.arange(384)
    fold_to = jnp.where(lane < 256, lane // 128, 2) * RANK + lane % RANK
    fold = (fold_to[:, None] == jnp.arange(128)[None, :]).astype(BF16)

    gu_out, down_out = call(
        unpack_kernel,
        [shape(128, 4096, dtype=BF16), shape(128, D, dtype=BF16)],
        [mlp_set[:, 6528:]],
        scratch=[pltpu.VMEM((D, 128), F32)],
        vmem=12,
    )

    hidden, normed_mlp = call(
        hidden_kernel,
        [shape(TOK, D), shape(TOK, D, dtype=BF16)],
        [place, x_own, part[:TOK], other_core(part[TOK:]), gain_mlp],
        specs=[SMEM] + [None] * 4,
        vmem=10,
    )

    pick4 = jnp.concatenate(
        [jnp.broadcast_to(picks_at(ahead, c), (TOK, 128)) for ahead in (3, 1, 0, 2)]
    )
    dm, turned = call(
        turn_kernel, [shape(512, D, dtype=BF16), shape(D, 512, dtype=BF16)], [cot]
    )
    n1, n3, n2 = from_x(normed_mlp)
    t2 = lax.all_gather(after(t2, mlp_set, n2), NATURAL, axis=0, tiled=True)
    dm = after(dm, n1, n2, n3)
    d_act, d_small_down = tiled_call(
        d_act_kernel,
        [shape(512, 2048), shape(512, 128, dtype=BF16)],
        [dm, turned, down_out, mlp_set, pick4, mlp_set],
        [
            whole_spec(512, D),
            whole_spec(D, 512),
            whole_spec(128, D),
            pl.BlockSpec((512, 128), lambda i: (i, 50)),
            whole_spec(512, 128),
            pl.BlockSpec((512, 2048), lambda i: (i, 2)),
        ],
        [pl.BlockSpec((512, 512), lambda i: (0, i)), whole_spec(512, 128)],
        flops=2 * 512 * 2048 * D,
        vmem=52,
    )

    def feed(part, n, g_gate, g_up):
        lines = pl.BlockSpec((16, 4, 8, 128), lambda i: (0, i, 0, 0))
        return tiled_call(
            feed_kernel,
            [
                shape(256, 2048, dtype=BF16),
                shape(256, D + 384, dtype=BF16),
                shape(16, 16, 8, 128),
                shape(16, 16, 8, 128),
            ],
            [n, d_act, pick4, mlp_set, mlp_set, gu_out, gu_out, mlp_set, mlp_set, g_gate, g_up],
            [
                whole_spec(256, D),
                pl.BlockSpec((256, 512), lambda i: (part, i)),
                pl.BlockSpec((256, 128), lambda i: (part, 0)),
                pl.BlockSpec((D, 512), lambda i: (0, i)),
                pl.BlockSpec((D, 512), lambda i: (0, i + 4)),
                pl.BlockSpec((128, 512), lambda i: (0, i)),
                pl.BlockSpec((128, 512), lambda i: (0, i + 4)),
                block(D, 256, 24),
                pl.BlockSpec((512, 128), lambda i: (i, 50)),
                lines,
                lines,
            ],
            [pl.BlockSpec((256, 512), lambda i: (0, i)), whole_spec(256, D + 384), lines, lines],
            [pltpu.VMEM((D + 384, 256), F32), pltpu.VMEM((256, 256), BF16)],
            flops=2 * 256 * 4096 * D * 2,
            vmem=52,
        )

    none = jnp.zeros((16, 16, 8, 128), F32)
    act_a, back_a, g_gate, g_up = feed(0, jnp.concatenate([n1, n3]), none, none)
    back = [along_x(back_a[:TOK], 3), along_x(back_a[TOK:], 1)]
    act_b, back_b, g_gate, g_up = feed(1, jnp.concatenate([normed_mlp, n2]), g_gate, g_up)
    back = [*back, back_b[:TOK], along_x(after(back_b[TOK:], back), 2)]

    gu_lines = 2.0 * jnp.concatenate([g_gate, g_up], axis=1).reshape(16, 256, 128)
    gu_lines = gu_lines.astype(BF16)
    d_hidden, d_attn, d_small_gu, small_down = call(
        d_hidden_kernel,
        [
            shape(TOK, D),
            shape(TOK, D, dtype=BF16),
            shape(TOK, 256, dtype=BF16),
            shape(TOK, 128, dtype=BF16),
        ],
        [hidden, cot_own, gain_mlp, *back, mlp_set, pick_f],
        specs=[None] * 7 + [block(D, 256, 24), None],
        vmem=52,
    )

    mine, theirs, d_small_o, halves = call(
        project_back_kernel,
        [
            shape(256, 1024),
            shape(256, 1024, dtype=BF16),
            shape(256, 128, dtype=BF16),
            shape(256, 1024, dtype=BF16),
        ],
        [place, d_attn, other_core(d_attn), o_whole, o_whole, out_out, pick_f],
        specs=[SMEM, None, None, o_spec, oa_spec, None, None],
        flops=2 * 256 * D * 1024,
        vmem=20,
    )
    (send,) = call(
        pack_kernel, [shape(16, TOK, 128, dtype=BF16)], [mine, other_core(theirs)], vmem=6
    )

    down, g_down_in = tiled_call(
        down_kernel,
        [shape(512, D, dtype=BF16), shape(2048, 128, dtype=BF16)],
        [after(act_a, send), act_b, d_small_down, mlp_set],
        [
            pl.BlockSpec((256, 512), lambda i: (0, i)),
            pl.BlockSpec((256, 512), lambda i: (0, i)),
            whole_spec(512, 128),
            pl.BlockSpec((512, 2048), lambda i: (i, 2)),
        ],
        [whole_spec(512, D), pl.BlockSpec((512, 128), lambda i: (i, 0))],
        [pltpu.VMEM((512, D), F32)],
        flops=2 * 512 * 2048 * D,
        vmem=52,
    )
    down = after(down, d_attn)
    down = [
        along_x(down[:TOK], 3),
        along_x(down[TOK : 2 * TOK], 1),
        down[2 * TOK : 3 * TOK],
        along_x(down[3 * TOK :], 2),
    ]
    d_out = a2a(send, BLOCKS).reshape(GTOK, 128)
    (early,) = call(
        early_grads_kernel,
        [shape(16, 640, 128, dtype=BF16)],
        [
            gu_lines,
            g_down_in,
            after(d_small_gu, send),
            normed_mlp,
            small_down,
            cot_own,
            d_small_o,
            attended,
            small_o,
            halves,
            fold,
        ],
        scratch=[pltpu.VMEM((16, 384, 128), F32)],
        vmem=28,
    )
    early = a2a(after(early, d_out), NATURAL)
    q_out, k_out, v_out = call(
        unpack_qkv_kernel,
        [shape(128, 1024, dtype=BF16), shape(128, 512, dtype=BF16), shape(128, 512, dtype=BF16)],
        [t2[:, 1536:]],
        scratch=[pltpu.VMEM((D, 128), F32)],
        vmem=8,
    )
    (dz,) = call(
        attend_back_kernel,
        [shape(GTOK, 256, dtype=BF16)],
        [after(z, q_out), d_out, stat],
        scratch=[pltpu.VMEM((GTOK, HDIM), F32), pltpu.VMEM((GTOK, HDIM), F32)],
        flops=5 * 2 * 2 * 30 * CLEN * CLEN * HDIM * 4,
        vmem=24,
    )
    parts = a2a(after(dz, down, early).reshape(16, TOK, 256), BLOCKS)
    (output,) = call(
        output_kernel,
        [shape(TOK, D, dtype=BF16)],
        [after(hidden, dz), *down, down_out, small_down],
        vmem=12,
    )
    output = swap_mid(output)
    plane, g_down_in = call(
        sums_kernel,
        [shape(8, 120, 128), shape(128, 128)],
        [after(source_slot, dz), early],
        scratch=[pltpu.VMEM((512, 128), F32), pltpu.VMEM((256, 128), F32)],
        specs=[SMEM, None],
        vmem=12,
    )
    plane = plane.reshape(4, 2, 120, 128)

    def to_chip(k):
        return lax.dynamic_index_in_dim(plane, (x + k) % 4, 0, keepdims=False)

    by_chip = jnp.stack([to_chip(0)] + [along_x(to_chip(k), k) for k in (1, 2, 3)])
    keep = lax.dynamic_index_in_dim(by_chip, c, 1, keepdims=False)
    take = other_core(lax.dynamic_index_in_dim(by_chip, 1 - c, 1, keepdims=False))

    parts = after(parts, keep, take)
    d_joint, mine_small, their_small = call(
        qkv_back_kernel,
        [shape(256, 1536, dtype=BF16), shape(TOK, 384), shape(TOK, 384, dtype=BF16)],
        [parts, q_out, k_out, v_out, cq, sq, ckv, skv],
        vmem=12,
    )
    d_small_qkv, late = call(
        late_grads_kernel,
        [shape(TOK, 384, dtype=BF16), shape(D, 256, dtype=BF16)],
        [mine_small, other_core(their_small), pick_f, normed_attn, small_qkv, d_joint, fold],
        scratch=[pltpu.VMEM((D, 128), F32)],
        vmem=14,
    )
    mine, theirs = call(
        d_normed_kernel,
        [shape(TOK, D), shape(TOK, D, dtype=BF16)],
        [after(d_joint, late), t2],
        specs=[None, w_spec],
        flops=2 * 256 * D * 1536,
        vmem=20,
    )
    late = a2a(late.reshape(128, 16, 256), NATURAL + PLANE)
    (input_grad,) = call(
        last_kernel,
        [shape(TOK, D, dtype=BF16)],
        [x_own, d_hidden, gain_attn, mine, other_core(theirs), d_small_qkv, heads],
        specs=[None] * 6 + [block(D, 384, 1)],
        vmem=14,
    )
    input_grad = swap_mid(input_grad)

    late_first, late_second = call(
        late_sums_kernel,
        [shape(8, 16, 128), shape(2, 16, 128)],
        [device_slot, late],
        specs=[SMEM, None],
        vmem=8,
    )
    both = keep + take
    gu = [
        lax.dynamic_index_in_dim(both[:, :32], (x - k) % 4, 0, keepdims=False) for k in range(4)
    ]
    gu = jnp.stack(gu).reshape(4, 2, 2, 2, 4, 128).transpose(1, 3, 2, 4, 0, 5)
    grad_gu_out = gu.reshape(1, 2 * UNITS)
    half = g_down_in.reshape(2, 64, 128)
    to_other = lax.dynamic_index_in_dim(half, 1 - c, 0, keepdims=False)
    grad_down_in = lax.dynamic_index_in_dim(half, c, 0, keepdims=False)
    grad_down_in = swap_mid(grad_down_in + other_core(to_other))
    total = jnp.sum(both[:, 32:112], axis=0)
    first = total[:64].reshape(4, 16, 2, 4, RANK).transpose(1, 3, 0, 2, 4).reshape(16, 4, 128)
    grad_gu_in = swap_mid(first[:, :2]).reshape(16, 256)
    grad_out_in = swap_mid(first[:, 2])
    grad_down_out = swap_mid(total[64:80].reshape(1, D))
    keep, take = jnp.sum(keep[:, 112:], axis=0), jnp.sum(take[:, 112:], axis=0)
    halves = jnp.where(c == 0, jnp.stack([keep, take]), jnp.stack([take, keep]))
    grad_out_out = swap_mid(halves.reshape(1, D))
    first = late_first[:, :, :48].reshape(8, 16, 3, RANK).transpose(1, 2, 0, 3)
    grad_qkv_in = swap_mid(first.reshape(16, 3, 128)).reshape(16, 384)
    grad_q_out = swap_mid(late_second[:, :8].reshape(1, D))
    kv = late_second[:, 8:12].reshape(2, 4, 2, HDIM).transpose(2, 0, 1, 3).reshape(2, 512)
    grad_kv_out = swap_mid(kv).reshape(1, 1024)

    return (
        output[None],
        input_grad[None],
        grad_qkv_in,
        grad_q_out,
        grad_kv_out,
        grad_out_in,
        grad_out_out,
        grad_gu_in,
        grad_gu_out,
        grad_down_in,
        grad_down_out,
    )


def solution(mesh):
    fine = Mesh(mesh.devices.reshape(2, 2, 4, 4, 2), AXES)
    tok = P(PLANE, BLOCKS, None)
    flat = P(AXES)
    rows = P(AXES, None)
    return jax.shard_map(
        local,
        mesh=fine,
        in_specs=(tok, P(PLANE, None), flat, flat) + (rows,) * 13 + (tok,),
        out_specs=(tok, tok) + (rows,) * 9,
        check_vma=False,
    )
```

```python
import functools

import jax
import jax.numpy as jnp
from jax import lax
from jax.experimental import pallas as pl
from jax.experimental.pallas import tpu as pltpu
from jax.sharding import Mesh
from jax.sharding import PartitionSpec as P

HEADS = 32
KVH = 8
HDIM = 64
D = HEADS * HDIM
UNITS = 8192
PROMPT = 1024
CLEN = 256
GTOK = 2048
TOK = 128
RANK = 16

EPS = 1e-5
SKIP = 0.22
ROPE_BASE = 10000000.0
NEG = -1e30

F32 = jnp.float32
BF16 = jnp.bfloat16

AXES = ("zl", "zh", "y", "x", "c")
BLOCKS = ("zl", "zh", "y")
NATURAL = ("zh", "zl", "y")
PLANE = ("x", "c")

def mm(a, b):
    return jnp.dot(a, b, preferred_element_type=F32)


def mm_nt(a, b):
    return lax.dot_general(a, b, (((1,), (1,)), ((), ())), preferred_element_type=F32)


def mm_tn(a, b):
    return lax.dot_general(a, b, (((0,), (0,)), ((), ())), preferred_element_type=F32)


def swap_mid(v, axis=-1):
    axis = axis % v.ndim
    n = v.shape[axis] // 4
    q = [lax.slice_in_dim(v, k * n, (k + 1) * n, axis=axis) for k in (0, 2, 1, 3)]
    return jnp.concatenate(q, axis=axis)


def a2a(v, axes):
    return lax.all_to_all(v, axes, 0, 0, tiled=True)


def other_core(v):
    return lax.ppermute(v, "c", [(0, 1), (1, 0)])


def along_x(v, k):
    return lax.ppermute(v, "x", [(i, (i + k) % 4) for i in range(4)])


MIB = 1024 * 1024


def nbytes(arrays):
    return sum(a.size * a.dtype.itemsize for a in arrays)


def job(g, j):
    return (j // 2) * 4 + g * 2 + j % 2


def far_of(one, three):
    half = one.shape[0] // 2
    return jnp.concatenate([along_x(one[:half], 1), along_x(three[half:], 3)])


def from_x(v):
    one, three = along_x(v, 1), along_x(v, 3)
    return one, three, far_of(one, three)


def call(kernel, outs, args, scratch=(), specs=None, flops=0, vmem=24, deps=()):
    if specs is None:
        specs = [None] * len(args)
    ins = [pl.BlockSpec(memory_space=pltpu.VMEM) if s is None else s for s in specs]
    ins = ins + [pl.BlockSpec(memory_space=pl.ANY)] * len(deps)
    return pl.pallas_call(
        ignoring(kernel, len(args), len(deps)),
        name=kernel.__name__,
        grid=(1,),
        out_shape=outs,
        in_specs=ins,
        out_specs=[pl.BlockSpec(memory_space=pltpu.VMEM)] * len(outs),
        scratch_shapes=list(scratch),
        compiler_params=pltpu.CompilerParams(vmem_limit_bytes=vmem * MIB),
        cost_estimate=pl.CostEstimate(
            flops=flops, bytes_accessed=nbytes(args) + nbytes(outs), transcendentals=0
        ),
    )(*args, *deps)


def tiled_call(
    kernel, outs, args, specs, out_specs, scratch=(), flops=0, steps=4, vmem=32, deps=()
):
    size = nbytes(outs) + 2 * flops // 1024
    return pl.pallas_call(
        ignoring(kernel, len(args), len(deps)),
        name=kernel.__name__,
        grid=(steps,),
        out_shape=outs,
        in_specs=specs + [pl.BlockSpec(memory_space=pl.ANY)] * len(deps),
        out_specs=out_specs,
        scratch_shapes=list(scratch),
        compiler_params=pltpu.CompilerParams(vmem_limit_bytes=vmem * MIB),
        cost_estimate=pl.CostEstimate(flops=flops, bytes_accessed=size, transcendentals=0),
    )(*args, *deps)


def shape(*dims, dtype=F32):
    return jax.ShapeDtypeStruct(dims, dtype)


def block(rows, cols, index):
    return pl.BlockSpec((rows, cols), lambda i: (0, index), pipeline_mode=pl.Buffered(1))


def once(rows, cols):
    return pl.BlockSpec((rows, cols), lambda i: (0, 0), pipeline_mode=pl.Buffered(1))


def whole_spec(rows, cols):
    return pl.BlockSpec((rows, cols), lambda i: (0, 0))


def ignoring(kernel, first, count):
    def body(*refs):
        kernel(*refs[:first], *refs[first + count :])

    return body


def gate(v, *deps):
    def copy(ref, out):
        out[...] = ref[...]

    return call(copy, [jax.ShapeDtypeStruct(v.shape, v.dtype)], [v], deps=deps, vmem=8)[0]


def segment_of(block_index):
    return jnp.where(block_index < 8, 0, 1 + (block_index - 8) // 2)


SMEM = pl.BlockSpec(memory_space=pltpu.SMEM)


def rope(t, cos, sin):
    lane = lax.broadcasted_iota(jnp.int32, t.shape, 1) % HDIM
    partner = jnp.where(lane < HDIM // 2, pltpu.roll(t, 96, 1), pltpu.roll(t, 32, 1))
    return t * cos + partner * sin


def assemble(x, pieces, whole):
    for piece, ahead in zip(pieces, (0, 3, 1, 2)):
        at = lax.rem(x + ahead, 4) * 32

        def place(i, _, piece=piece, at=at):
            to = pl.multiple_of(i * 128 + at, 32)
            whole[pl.ds(to, 32), :] = piece[pl.ds(pl.multiple_of(i * 32, 32), 32), :]
            return 0

        lax.fori_loop(0, 16, place, 0)


def gain_row(g, first):
    lane = lax.broadcasted_iota(jnp.int32, (128, 128), 1)
    row = lax.broadcasted_iota(jnp.int32, (128, 128), 0)
    tiled = mm(g.astype(BF16), (row == first + lane % 16).astype(BF16))
    tiled = jnp.where(lane // 16 == row % 8, tiled, 0.0).astype(BF16)
    to_row = lax.broadcasted_iota(jnp.int32, (16, 128), 1) // 8
    to_row = (to_row == lax.broadcasted_iota(jnp.int32, (16, 128), 0)).astype(BF16)
    rows = mm(to_row, tiled)
    return jnp.concatenate([rows[k : k + 1] for k in range(16)], axis=1)


def only_keys(kv):
    lane = lax.broadcasted_iota(jnp.int32, kv.shape, 1) % 128
    return jnp.where(lane < HDIM, kv, 0.0).astype(BF16), jnp.where(lane < HDIM, 0.0, kv).astype(BF16)


def qkv_kernel(
    place, x, e, pick, cq, sq, ckv, skv, send, normed, small, gain, gain_mlp, n, s_all, wide
):
    core = place[1]
    wide[...] = e[:, 768:896].astype(F32)
    q_out = jnp.concatenate([wide[pl.ds(t, 128, stride=16), :] for t in range(2)], axis=1)
    q_out = q_out.astype(BF16)
    k_out, v_out = only_keys(wide[pl.ds(2, 128, stride=16), :])
    gain[...] = gain_row(wide[pl.ds(3, 128, stride=16), :], 0)
    gain_mlp[...] = gain_row(wide[pl.ds(3, 128, stride=16), :], 16)
    for k in range(4):
        rows = slice(2 * k * TOK, (2 * k + 2) * TOK)
        v = x[rows, :].astype(F32)
        r = lax.rsqrt(jnp.mean(v * v, axis=1, keepdims=True) + EPS)
        n[rows, :] = (v * r * gain[...]).astype(BF16)
        s = mm(n[rows, :], e[:, 384:768]).astype(BF16)
        s = jnp.concatenate(
            [s[:TOK] * pick[2 * k : 2 * k + 1, :], s[TOK:] * pick[2 * k + 1 : 2 * k + 2, :]], axis=0
        )
        s_all[rows, :] = s
        q = mm(n[rows, :], e[:, :256]) + 2.0 * mm(s[:, :128], q_out)
        kv = mm(n[rows, :], e[:, 256:384]) + 2.0 * (
            mm(s[:, 128:256], k_out) + mm(s[:, 256:], v_out)
        )
        for o in range(2):
            here = slice(o * TOK, (o + 1) * TOK)
            t = rope(kv[here], ckv[...], skv[...]).astype(BF16)
            at = k * 4 + 2 * lax.rem(core + o, 2)
            for j in range(2):
                p = rope(q[here, j * 128 : (j + 1) * 128], cq[...], sq[...]).astype(BF16)
                send[at + j, :, 0:128] = p
                send[at + j, :, 128:256] = t
    own = pl.multiple_of((2 * place[0] + core) * TOK, TOK)
    other = pl.multiple_of((2 * place[0] + 1 - core) * TOK, TOK)
    normed[...] = n[pl.ds(own, TOK), :]
    small[:TOK, :] = s_all[pl.ds(own, TOK), :]
    small[TOK:, :] = s_all[pl.ds(other, TOK), :]


def heads_of(ref, rows, scale=None):
    t = ref[rows, :128]
    both = jnp.concatenate([t[:, :HDIM], t[:, HDIM:]], axis=0)
    return both if scale is None else both * jnp.asarray(scale, BF16)


def allowed_in_block():
    key = lax.broadcasted_iota(jnp.int32, (CLEN, 2 * CLEN), 0)
    query = lax.broadcasted_iota(jnp.int32, (CLEN, 2 * CLEN), 1) % CLEN
    return key <= query


def attend_kernel(z, out, stat):
    allowed = allowed_in_block()
    for i in range(GTOK // CLEN):
        rows = slice(i * CLEN, (i + 1) * CLEN)
        full = min(i, PROMPT // CLEN) * CLEN
        q = heads_of(z, rows, 1.0 / 64.0)
        sd = jnp.where(allowed, mm_nt(z[rows, 128:192], q), NEG)
        top = jnp.max(sd, axis=0, keepdims=True)
        if full:
            sf = mm_nt(z[0:full, 128:192], q)
            top = jnp.maximum(top, jnp.max(sf, axis=0, keepdims=True))
        pd = jnp.exp(sd - top)
        total = jnp.sum(pd, axis=0, keepdims=True)
        o = mm_tn(z[rows, 192:256], pd.astype(BF16))
        if full:
            pf = jnp.exp(sf - top)
            total = total + jnp.sum(pf, axis=0, keepdims=True)
            o = o + mm_tn(z[0:full, 192:256], pf.astype(BF16))
        o = o / total
        stat[i : i + 1, :] = top + jnp.log(total)
        both = jnp.concatenate([o[:, :CLEN], o[:, CLEN:]], axis=0)
        out[rows, :] = both.T.astype(BF16)


def attend_back_kernel(z, d_out, stat, dz, dk, dv):
    allowed = allowed_in_block()
    dk[...] = jnp.zeros_like(dk)
    dv[...] = jnp.zeros_like(dv)
    for i in range(GTOK // CLEN):
        rows = slice(i * CLEN, (i + 1) * CLEN)
        full = min(i, PROMPT // CLEN) * CLEN
        q = heads_of(z, rows, 1.0 / 64.0)
        do = heads_of(d_out, rows)
        lse = stat[i : i + 1, :]
        kd = z[rows, 128:192]
        pd = jnp.exp(jnp.where(allowed, mm_nt(kd, q), NEG) - lse)
        dpd = mm_nt(z[rows, 192:256], do)
        inner = jnp.sum(pd * dpd, axis=0, keepdims=True)
        if full:
            kf = z[0:full, 128:192]
            pf = jnp.exp(mm_nt(kf, q) - lse)
            dpf = mm_nt(z[0:full, 192:256], do)
            inner = inner + jnp.sum(pf * dpf, axis=0, keepdims=True)
        dsd = (pd * (dpd - inner)).astype(BF16)
        dq = mm_tn(kd, dsd)
        dk[rows, :] += mm(dsd, q)
        dv[rows, :] += mm(pd.astype(BF16), do)
        if full:
            dsf = (pf * (dpf - inner)).astype(BF16)
            dq = dq + mm_tn(kf, dsf)
            dk[0:full, :] += mm(dsf, q)
            dv[0:full, :] += mm(pf.astype(BF16), do)
        dq = dq * (1.0 / 64.0)
        both = jnp.concatenate([dq[:, :CLEN], dq[:, CLEN:]], axis=0)
        dz[rows, 0:128] = both.T.astype(BF16)
    dz[:, 128:256] = jnp.concatenate([dk[...], dv[...]], axis=1).astype(BF16)


def project_kernel(
    place, mine, theirs, e0, e1, e2, e3, pick,
    part, their_part, small, attended, whole, a_out, att, wide,
):
    assemble(place[0], (e0, e1, e2, e3), whole)
    wide[...] = whole[:, 1152:1280].astype(F32)
    for t in range(16):
        a_out[:, t * 128 : (t + 1) * 128] = wide[pl.ds(t, 128, stride=16), :].astype(BF16)
    c = place[1]
    here = pl.multiple_of(c * 1024, 1024)
    there = pl.multiple_of((1 - c) * 1024, 1024)
    for g in range(2):
        rows = slice(g * TOK, (g + 1) * TOK)
        for j in range(8):
            cols = slice(j * 128, (j + 1) * 128)
            att[0, rows, cols] = mine[job(g, j)]
            att[1, rows, cols] = theirs[job(1 - g, j)]
    m, t = att[0], att[1]
    attended[:, pl.ds(here, 1024)] = m[:TOK]
    attended[:, pl.ds(there, 1024)] = t[:TOK]
    s = mm(m, whole[pl.ds(here, 1024), 1024:1152]) + mm(t, whole[pl.ds(there, 1024), 1024:1152])
    s = s.astype(BF16)
    s = jnp.concatenate([s[:TOK] * pick[0:1, :128], s[TOK:] * pick[1:2, :128]], axis=0)
    small[...] = s
    both = (
        mm(m, whole[pl.ds(here, 1024), :1024])
        + mm(t, whole[pl.ds(there, 1024), :1024])
        + 2.0 * mm(s, a_out[:, pl.ds(here, 1024)])
    )
    part[...] = both[:TOK]
    their_part[...] = both[TOK:]


def hidden_kernel(place, x, mine, theirs, gain, hidden, normed):
    c = place[1]
    here = pl.multiple_of(c * 1024, 1024)
    there = pl.multiple_of((1 - c) * 1024, 1024)
    hidden[:, pl.ds(here, 1024)] = SKIP * mine[...]
    hidden[:, pl.ds(there, 1024)] = SKIP * theirs[...]
    h = x[...].astype(F32) + hidden[...]
    hidden[...] = h
    r = lax.rsqrt(jnp.mean(h * h, axis=1, keepdims=True) + EPS)
    normed[...] = (h * r * gain[...]).astype(BF16)


def halves_kernel(one, three, half_one, half_three):
    half_one[...] = one[: TOK // 2, :]
    half_three[...] = three[TOK // 2 :, :]


def unpack_kernel(outs, gu_out, down_out, wide):
    for k in range(3):
        wide[...] = outs[:, k * 128 : (k + 1) * 128].astype(F32)
        for t in range(16):
            at = (3 * t + k) * 128
            part = wide[pl.ds(t, 128, stride=16), :].astype(BF16)
            if at < 4096:
                gu_out[:, at : at + 128] = part
            else:
                down_out[:, at - 4096 : at - 3968] = part


def turn_kernel(cot, dm, turned):
    d = (SKIP * cot[...].astype(F32)).astype(BF16)
    dm[...] = d
    turned[...] = d.T


def d_act_kernel(dm, turned, a_out, a_in, pick, w, d_act, small):
    @pl.when(pl.program_id(0) == 0)
    def _():
        s = 2.0 * mm_nt(dm[...], a_out[...]) * pick[...].astype(F32)
        small[...] = s.astype(BF16)

    d_act[...] = mm(w[...], turned[...]).T + mm_nt(small[...], a_in[...])


def feed_kernel(
    n_one, n_two, d_act, pick, w_gate, w_up, o_gate, o_up, a_in, a_down, g_gate0, g_up0,
    act, back, back1, g_gate, g_up, total, small, n,
):
    step = pl.program_id(0)

    @pl.when(step == 0)
    def _():
        n[:TOK, :] = n_one[...]
        n[TOK:, :] = n_two[...]
        s = mm(n[...], a_in[...]).astype(BF16)
        p = pick[...]
        small[...] = s * jnp.concatenate([p, p], axis=1)
        total[...] = jnp.zeros_like(total)

    x = n[...]
    gate = mm(x, w_gate[...]) + 2.0 * mm(small[:, :128], o_gate[...])
    up = mm(x, w_up[...]) + 2.0 * mm(small[:, 128:], o_up[...])
    sg = 1.0 / (1.0 + jnp.exp(-gate))
    gs = gate * sg
    act[...] = (gs * up).astype(BF16)
    da = d_act[...]
    dg = (da * up * (sg + gs * (1.0 - sg))).astype(BF16)
    du = (da * gs).astype(BF16)
    total[:D, :] += mm_nt(w_gate[...], dg) + mm_nt(w_up[...], du)
    total[D : D + 128, :] += mm_nt(o_gate[...], dg)
    total[D + 128 : D + 256, :] += mm_nt(o_up[...], du)
    total[D + 256 :, :] += mm_nt(a_down[...].T, act[...])
    for t in range(4):
        cols = slice(t * 128, (t + 1) * 128)
        g = mm_tn(small[:, :128], dg[:, cols]).reshape(16, 8, 128)
        g_gate[:, t] = g_gate0[:, t] + g
        g = mm_tn(small[:, 128:], du[:, cols]).reshape(16, 8, 128)
        g_up[:, t] = g_up0[:, t] + g

    @pl.when(step == pl.num_programs(0) - 1)
    def _():
        back[...] = total[:, :TOK].T.astype(BF16)
        back1[...] = total[:, TOK:].T.astype(BF16)


def down_kernel(act_a, act_b, d_small, w, out, out1, out2, out3, g_in, total):
    step = pl.program_id(0)

    @pl.when(step == 0)
    def _():
        total[...] = jnp.zeros_like(total)

    for k, act in enumerate((act_a, act_b)):
        rows = slice(k * 256, (k + 1) * 256)
        total[rows, :] += mm(act[...], w[...])
    g = mm_tn(act_a[...], d_small[:256]) + mm_tn(act_b[...], d_small[256:])
    g_in[...] = g.astype(BF16)

    @pl.when(step == pl.num_programs(0) - 1)
    def _():
        for k, ref in enumerate((out, out1, out2, out3)):
            ref[...] = total[k * TOK : (k + 1) * TOK, :].astype(BF16)


def output_kernel(hidden, p0, p1, p2, p3, a_out, small, out):
    total = p0[...].astype(F32) + p1[...].astype(F32) + p2[...].astype(F32) + p3[...].astype(F32)
    out[...] = (hidden[...] + SKIP * (total + 2.0 * mm(small[...], a_out[...]))).astype(BF16)


def rms_back(v, gain, e):
    r = lax.rsqrt(jnp.mean(v * v, axis=1, keepdims=True) + EPS)
    we = gain * e
    return r * we - v * (r * r * r) * jnp.mean(v * we, axis=1, keepdims=True)


def d_hidden_kernel(
    hidden, cot, gain, p0, p1, p2, p3, a_in, pick, d_hidden, d_attn, small, small_down
):
    total = p0[...].astype(F32) + p1[...].astype(F32) + p2[...].astype(F32) + p3[...].astype(F32)
    s = (2.0 * total[:, D : D + 256] * pick[0:1, :256]).astype(BF16)
    small[...] = s
    small_down[...] = (total[:, D + 256 :] * pick[0:1, :128]).astype(BF16)
    e = total[:, :D] + mm_nt(s, a_in[...])
    d = cot[...].astype(F32) + rms_back(hidden[...], gain[...], e)
    d_hidden[...] = d
    d_attn[...] = (SKIP * d).astype(BF16)


def project_back_kernel(place, own, other, w, a_in, a_out, pick, mine, theirs, small, halves):
    c = place[1]
    here = pl.multiple_of(c * 1024, 1024)
    there = pl.multiple_of((1 - c) * 1024, 1024)
    full = jnp.concatenate([own[...], other[...]], axis=0)
    s = 2.0 * mm_nt(full, a_out[...])
    s = jnp.concatenate([s[:TOK] * pick[0:1, :128], s[TOK:] * pick[1:2, :128]], axis=0)
    s = s.astype(BF16)
    small[...] = s
    half = jnp.concatenate([own[:, pl.ds(here, 1024)], other[:, pl.ds(here, 1024)]], axis=0)
    halves[...] = half
    theirs[...] = mm_nt(half, w[pl.ds(there, 1024), :]).astype(BF16)
    mine[...] = mm_nt(half, w[pl.ds(here, 1024), :]) + mm_nt(s, a_in[pl.ds(here, 1024), :])


def pack_kernel(mine, theirs, send):
    for g in range(2):
        rows = slice(g * TOK, (g + 1) * TOK)
        swapped = slice((1 - g) * TOK, (2 - g) * TOK)
        for j in range(8):
            cols = slice(j * 128, (j + 1) * 128)
            send[job(g, j)] = (mine[rows, cols] + theirs[swapped, cols].astype(F32)).astype(BF16)


def early_grads_kernel(
    g_down_in, d_small_gu, normed, small_down, cot, d_small_o, attended, small_o, halves, fold,
    out, lines,
):
    f = mm(d_small_gu[...], fold[:256, :]).astype(BF16)[:, :HDIM]
    g = mm_tn(f, normed[...])
    f = mm(d_small_o[:TOK], fold[256:384, :]).astype(BF16)[:, :HDIM]
    g = g + mm_tn(f, attended[...])
    dm = (SKIP * cot[...].astype(F32)).astype(BF16)
    g_down = 2.0 * mm_tn(small_down[...], dm)
    g_o = 2.0 * mm_tn(small_o[...], halves[...])
    for k in range(16):
        lines[k, 128:192, :] = g[:, k * 128 : (k + 1) * 128]
        rows = slice(k * 8, (k + 1) * 8)
        for t in range(16):
            lines[k, 192 + t * 8 : 200 + t * 8, :] = g_down[rows, t * 128 : (t + 1) * 128]
        for t in range(8):
            lines[k, 320 + t * 8 : 328 + t * 8, :] = g_o[rows, t * 128 : (t + 1) * 128]
        out[k, :128, :] = g_down_in[k * 128 : (k + 1) * 128, :]
        out[k, 128:, :] = lines[k, 128:, :].astype(BF16)


def sums_kernel(slot, gu, early, plane, g_down_in, first, total):
    first[...] = jnp.zeros_like(first)
    total[...] = gu[0].astype(F32)
    for k in range(1, 16):
        total[...] += gu[k].astype(F32)
    for r in range(8):
        plane[r, 0:32, :] = total[pl.ds(r, 32, stride=8), :]
    d = early[0, :128, :].astype(F32)
    o = early[0, 192:384, :].astype(F32)
    for k in range(16):
        at = pl.multiple_of(slot[k] * HDIM, HDIM)
        first[pl.ds(at, HDIM), :] += early[k, 128:192, :].astype(F32)
        if k:
            d = d + early[k, :128, :].astype(F32)
            o = o + early[k, 192:384, :].astype(F32)
    g_down_in[...] = d
    total[:192, :] = o
    turned = first[...].T
    for r in range(8):
        for k in range(4):
            part = turned[r * 16 : (r + 1) * 16, k * 128 : (k + 1) * 128]
            plane[r, 32 + k * 16 : 48 + k * 16, :] = part
        plane[r, 96:120, :] = total[pl.ds(r, 24, stride=8), :]


def unpack_qkv_kernel(outs, q_out, k_out, v_out, wide):
    wide[...] = outs[...].astype(F32)
    q = [wide[pl.ds(t, 128, stride=16), :] for t in range(8)]
    q_out[...] = jnp.concatenate(q, axis=1).astype(BF16)
    kv = [wide[pl.ds(8 + t, 128, stride=16), :] for t in range(4)]
    k_out[...], v_out[...] = only_keys(jnp.concatenate(kv, axis=1))


def qkv_back_kernel(
    parts, q_out, k_out, v_out, cq, sq, ckv, skv, d_joint, mine_small, their_small
):
    for g in range(2):
        rows = slice(g * TOK, (g + 1) * TOK)
        for j in range(8):
            t = parts[job(g, j), :, 0:128].astype(F32)
            d_joint[rows, j * 128 : (j + 1) * 128] = rope(t, cq[...], -sq[...]).astype(BF16)
        for j in range(4):
            t = parts[job(g, 2 * j), :, 128:256].astype(F32)
            t = t + parts[job(g, 2 * j + 1), :, 128:256].astype(F32)
            d_joint[rows, 1024 + j * 128 : 1024 + (j + 1) * 128] = rope(
                t, ckv[...], -skv[...]
            ).astype(BF16)
    dq, dkv = d_joint[:, :1024], d_joint[:, 1024:]
    small = 2.0 * jnp.concatenate(
        [mm_nt(dq, q_out[...]), mm_nt(dkv, k_out[...]), mm_nt(dkv, v_out[...])], axis=1
    )
    mine_small[...] = small[:TOK]
    their_small[...] = small[TOK:].astype(BF16)


def late_grads_kernel(
    mine_small, their_small, pick, normed, small_qkv, d_joint, fold, small, out, g
):
    s = ((mine_small[...] + their_small[...].astype(F32)) * pick[0:1, :]).astype(BF16)
    small[...] = s
    f = mm(s, fold[...]).astype(BF16)
    out[:, :128] = mm_tn(normed[...], f).astype(BF16)
    gq = 2.0 * mm_tn(small_qkv[:, :128], d_joint[:, :1024])
    gk = mm_tn(small_qkv[:, 128:256], d_joint[:, 1024:])
    gv = mm_tn(small_qkv[:, 256:], d_joint[:, 1024:])
    lane = lax.broadcasted_iota(jnp.int32, gk.shape, 1) % 128
    gkv = 2.0 * jnp.where(lane < HDIM, gk, gv)
    for t in range(8):
        g[pl.ds(t, 128, stride=16), :] = gq[:, t * 128 : (t + 1) * 128]
    for t in range(4):
        g[pl.ds(8 + t, 128, stride=16), :] = gkv[:, t * 128 : (t + 1) * 128]
        g[pl.ds(12 + t, 128, stride=16), :] = jnp.zeros((128, 128), F32)
    out[:, 128:] = g[...].astype(BF16)


def late_sums_kernel(slot, late, first, second):
    first[...] = jnp.zeros_like(first)
    second[...] = jnp.zeros_like(second)

    def add(k, _):
        for core in range(2):
            v = late[2 * k + core].astype(F32)
            at = slot[2 * k + core]
            first[at] += v[:, :128]
            second[core] += v[:, 128:]
        return 0

    lax.fori_loop(0, 64, add, 0)


def d_normed_kernel(d_joint, w, mine, theirs):
    dn = mm_nt(d_joint[...], w[...])
    mine[...] = dn[:TOK]
    theirs[...] = dn[TOK:].astype(BF16)


def last_kernel(x, d_hidden, gain, mine, theirs, small, a, grad):
    dn = mine[...] + theirs[...].astype(F32) + mm_nt(small[...], a[...])
    v = x[...].astype(F32)
    grad[...] = (d_hidden[...] + rms_back(v, gain[...], dn)).astype(BF16)


def local(
    tokens,
    adapter_ids,
    norm_gain_attn,
    norm_gain_mlp,
    qkv_weight,
    output_projection_weight,
    gate_up_weight,
    down_projection_weight,
    qkv_adapter_in,
    q_adapter_out,
    kv_adapter_out,
    out_adapter_in,
    out_adapter_out,
    gate_up_adapter_in,
    gate_up_adapter_out,
    down_adapter_in,
    down_adapter_out,
    cotangent,
):
    c = lax.axis_index("c")
    x = lax.axis_index("x")
    b = lax.axis_index(BLOCKS)
    place = jnp.stack([x, c]).astype(jnp.int32)

    x_own = swap_mid(tokens[0])
    cot_own = swap_mid(cotangent[0])
    x_plane = lax.all_gather(x_own, PLANE, axis=0, tiled=True)

    q_w = swap_mid(qkv_weight[:, :D])
    k_w = swap_mid(qkv_weight[:, D : D + 512]).reshape(16, 8, 1, HDIM)
    v_w = swap_mid(qkv_weight[:, D + 512 :]).reshape(16, 8, 1, HDIM)
    kv_w = jnp.concatenate([k_w, v_w], axis=2).reshape(16, 1024)
    a_in = swap_mid(qkv_adapter_in.reshape(16, 3, 128)).reshape(16, 384)
    qo = swap_mid(q_adapter_out)
    ko = swap_mid(kv_adapter_out[:, :512]).reshape(8, 1, HDIM)
    vo = swap_mid(kv_adapter_out[:, 512:]).reshape(8, 1, HDIM)
    kvo = jnp.concatenate([ko, vo], axis=1).reshape(1, 1024)
    ids = adapter_ids[0]
    extra = jnp.concatenate([norm_gain_attn, norm_gain_mlp, ids.astype(BF16), jnp.zeros(91, BF16)])
    outs = jnp.concatenate(
        [
            qo.reshape(8, 2, 128),
            kvo.reshape(8, 1, 128),
            jnp.broadcast_to(extra, (8, 1, 128)),
            jnp.zeros((8, 12, 128), BF16),
        ],
        axis=1,
    )
    payload = jnp.concatenate(
        [
            q_w.reshape(16, 8, 256).transpose(1, 0, 2),
            kv_w.reshape(16, 8, 128).transpose(1, 0, 2),
            jnp.broadcast_to(a_in, (8, 16, 384)),
            outs,
        ],
        axis=2,
    )
    heads = payload.reshape(2, 4, 16, 896).transpose(1, 0, 2, 3).reshape(8, 16, 896)
    in_plane = a2a(heads, PLANE)
    ids_all = in_plane[:, 3, 800:805].astype(F32)
    heads = jnp.broadcast_to(in_plane.reshape(1, 128, 896), (16, 128, 896))
    heads = a2a(heads, NATURAL).reshape(D, 896)

    o_w = swap_mid(output_projection_weight).reshape(16, 2, 1024)
    o_out = swap_mid(out_adapter_out).reshape(16, 128)
    payload = jnp.concatenate(
        [
            o_w.transpose(1, 0, 2),
            jnp.broadcast_to(swap_mid(out_adapter_in), (2, 16, 128)),
            jnp.broadcast_to(o_out, (2, 16, 128)),
        ],
        axis=2,
    )

    def chip_rows(v):
        keep = lax.dynamic_index_in_dim(v, c, 0, keepdims=False)
        take = other_core(lax.dynamic_index_in_dim(v, 1 - c, 0, keepdims=False))
        return jnp.where(c == 0, jnp.concatenate([keep, take]), jnp.concatenate([take, keep]))

    chip = chip_rows(payload)
    o_mine = lax.all_gather(gate(chip, x_plane, in_plane), NATURAL, axis=0, tiled=True)
    o_set = [o_mine, *from_x(o_mine)]

    gu = gate_up_weight.reshape(16, 2, 2, 2, 4, 4, 128).transpose(5, 0, 1, 3, 2, 4, 6)
    gu = gu.reshape(4, 16, 4096)
    guo = gate_up_adapter_out.reshape(2, 2, 2, 4, 4, 128).transpose(4, 0, 2, 1, 3, 5)
    guo = guo.reshape(4, 4096)
    outs = jnp.concatenate([guo, jnp.broadcast_to(swap_mid(down_adapter_out), (4, D))], axis=1)
    gu_in = swap_mid(gate_up_adapter_in.reshape(16, 2, 128)).reshape(16, 256)
    to_x = jnp.concatenate(
        [
            gu,
            jnp.broadcast_to(gu_in, (4, 16, 256)),
            outs.reshape(4, 16, 384),
        ],
        axis=2,
    )

    to_x = gate(to_x, x_plane)

    def for_chip(k):
        return lax.dynamic_index_in_dim(to_x, (x + k) % 4, 0, keepdims=False)

    by_chip = [for_chip(0)] + [along_x(for_chip(k), k) for k in (1, 2, 3)]
    by_chip = jnp.stack(by_chip)

    def of_pair(core):
        two = [
            lax.dynamic_index_in_dim(by_chip, (x - 2 * core - j) % 4, 0, keepdims=False)
            for j in range(2)
        ]
        return jnp.stack(two)

    keep = of_pair(c)
    take = other_core(of_pair(1 - c))
    rows = jnp.where(c == 0, jnp.stack([keep, take], 1), jnp.stack([take, keep], 1))
    plane = rows.reshape(64, 4736)
    down_w = swap_mid(down_projection_weight)
    down_in = swap_mid(down_adapter_in)
    plane = jnp.concatenate(
        [plane[:, :4096], down_w, plane[:, 4096:4352], down_in, plane[:, 4352:]], axis=1
    )


    segment = segment_of(b)
    start = jnp.where(b < 8, b * TOK, PROMPT + ((b - 8) % 2) * TOK)
    positions = start + jnp.arange(TOK, dtype=jnp.int32)
    frequency = ROPE_BASE ** (-(jnp.arange(HDIM // 2, dtype=F32) * 2.0) / HDIM)
    angles = positions.astype(F32)[:, None] * frequency[None, :]
    cos, sin = jnp.cos(angles), jnp.sin(angles)
    one, zero = jnp.ones((TOK, HDIM), F32), jnp.zeros((TOK, HDIM), F32)
    cq = jnp.concatenate([cos] * 4, axis=1)
    sq = jnp.concatenate([-sin, sin, -sin, sin], axis=1)
    ckv = jnp.concatenate([cos, cos, one], axis=1)
    skv = jnp.concatenate([-sin, sin, zero], axis=1)

    col = jnp.arange(128)
    col_adapter = ((col >> 5) & 1) * 4 + ((col >> 6) & 1) * 2 + ((col >> 4) & 1)
    here = (jnp.arange(5) == segment).astype(F32)

    def picks(adapters):
        a = jnp.sum(adapters.astype(F32) * here)
        return (col_adapter.astype(F32) == a).astype(BF16)

    def picks_at(ahead, core):
        row = 2 * ((x + ahead) % 4) + core
        return picks(lax.dynamic_index_in_dim(ids_all, row, 0, keepdims=False))

    pick = jnp.stack([jnp.tile(picks(ids_all[k]), 3) for k in range(8)])
    pick_all = jnp.concatenate([pick, jnp.zeros((8, 384), BF16)], axis=0)
    pick = [lax.dynamic_slice_in_dim(pick, 2 * x + core, 1) for core in (c, 1 - c)]
    pick = jnp.concatenate([*pick, jnp.zeros((14, 384), BF16)], axis=0)
    pick_f = pick.astype(F32)

    send, normed_attn, small_qkv, gain_attn, gain_mlp = call(
        qkv_kernel,
        [
            shape(16, TOK, 256, dtype=BF16),
            shape(TOK, D, dtype=BF16),
            shape(256, 384, dtype=BF16),
            shape(1, D),
            shape(1, D),
        ],
        [place, x_plane, heads, pick_all, cq, sq, ckv, skv],
        deps=[plane],
        scratch=[
            pltpu.VMEM((1024, D), BF16),
            pltpu.VMEM((1024, 384), BF16),
            pltpu.VMEM((D, 128), F32),
        ],
        specs=[SMEM] + [None] * 7,
        flops=2 * 1024 * D * 768,
        vmem=40,
    )
    mlp_set = lax.all_gather(gate(plane, o_mine, send), NATURAL + ("c",), axis=0, tiled=True)
    z = a2a(a2a(send, "x"), BLOCKS).reshape(GTOK, 256)
    cot = [cot_own, *from_x(gate(cot_own, o_set[1]))]
    cot = jnp.concatenate([cot[1], cot[2], cot[0], cot[3]])

    t2 = jnp.concatenate(
        [
            q_w.reshape(16, 2, 1024).transpose(1, 0, 2),
            kv_w.reshape(16, 2, 512).transpose(1, 0, 2),
            jnp.concatenate(
                [qo.reshape(2, 8, 128), kvo.reshape(2, 4, 128), jnp.zeros((2, 4, 128), BF16)], axis=1
            ),
        ],
        axis=2,
    )
    t2 = chip_rows(t2)
    rel = jnp.stack([t2] + [along_x(t2, k) for k in (1, 2, 3)])
    rel = [lax.dynamic_index_in_dim(rel, (x - k) % 4, 0, keepdims=False) for k in range(4)]
    t2 = jnp.concatenate(rel)

    attended, stat = call(
        attend_kernel,
        [shape(GTOK, 128, dtype=BF16), shape(8, 512)],
        [z],
        deps=o_set[1:3],
        flops=2 * 2 * 2 * 30 * CLEN * CLEN * HDIM * 4,
        vmem=20,
    )
    mine = a2a(attended.reshape(16, TOK, 128), BLOCKS)
    theirs = other_core(mine)
    part, their_part, small_o, attended, o_whole, out_out = call(
        project_kernel,
        [
            shape(TOK, 1024),
            shape(TOK, 1024),
            shape(256, 128, dtype=BF16),
            shape(TOK, D, dtype=BF16),
            shape(D, 1280, dtype=BF16),
            shape(128, D, dtype=BF16),
        ],
        [place, mine, theirs, *o_set, pick],
        scratch=[pltpu.VMEM((2, 256, 1024), BF16), pltpu.VMEM((D, 128), F32)],
        specs=[SMEM] + [None] * 7,
        flops=2 * 256 * D * 1024,
        vmem=24,
    )
    w_spec = block(D, 1536, 0)
    o_spec = block(D, 1024, 0)
    oa_spec = block(D, 128, 8)

    device = jnp.arange(128)
    device_segment = segment_of(((device >> 5) & 1) * 8 + (device >> 6) * 4 + ((device >> 3) & 3))
    device_segment = (device_segment[:, None] == jnp.arange(5)).astype(F32)
    device_ids = jnp.broadcast_to(ids_all[None], (16, 8, 5)).reshape(128, 5)
    device_adapter = jnp.sum(device_ids * device_segment, axis=1)
    natural = device_adapter.astype(jnp.int32)
    device_slot = (natural >> 1 & 1) * 4 + (natural >> 2) * 2 + (natural & 1)
    source_slot = lax.dynamic_slice_in_dim(
        device_slot.reshape(16, 8).T.reshape(128), (2 * x + c) * 16, 16
    )
    lane = jnp.arange(384)
    fold_to = jnp.where(lane < 256, lane // 128, 2) * RANK + lane % RANK
    fold = (fold_to[:, None] == jnp.arange(128)[None, :]).astype(BF16)

    gu_out, down_out = call(
        unpack_kernel,
        [shape(128, 4096, dtype=BF16), shape(128, D, dtype=BF16)],
        [mlp_set[:, 6528:]],
        scratch=[pltpu.VMEM((D, 128), F32)],
        vmem=12,
    )

    hidden, normed_mlp = call(
        hidden_kernel,
        [shape(TOK, D), shape(TOK, D, dtype=BF16)],
        [place, x_own, part, other_core(their_part), gain_mlp],
        deps=[cot],
        specs=[SMEM] + [None] * 4,
        vmem=10,
    )

    pick4 = jnp.concatenate(
        [jnp.broadcast_to(picks_at(ahead, c), (TOK, 128)) for ahead in (3, 1, 0, 2)]
    )
    dm, turned = call(
        turn_kernel, [shape(512, D, dtype=BF16), shape(D, 512, dtype=BF16)], [cot]
    )
    n1, n3 = along_x(normed_mlp, 1), along_x(normed_mlp, 3)
    d_act, d_small_down = tiled_call(
        d_act_kernel,
        [shape(512, 2048), shape(512, 128, dtype=BF16)],
        [dm, turned, down_out, mlp_set, pick4, mlp_set],
        [
            whole_spec(512, D),
            whole_spec(D, 512),
            whole_spec(128, D),
            pl.BlockSpec((512, 128), lambda i: (i, 50)),
            whole_spec(512, 128),
            pl.BlockSpec((512, 2048), lambda i: (i, 2)),
        ],
        [pl.BlockSpec((512, 512), lambda i: (0, i)), whole_spec(512, 128)],
        flops=2 * 512 * 2048 * D,
        vmem=52,
    )

    half_one, half_three = call(
        halves_kernel,
        [shape(TOK // 2, D, dtype=BF16)] * 2,
        [n1, n3],
        deps=[d_act],
        vmem=6,
    )
    n2 = jnp.concatenate([along_x(half_one, 1), along_x(half_three, 3)])
    t2 = lax.all_gather(gate(t2, normed_mlp), NATURAL, axis=0, tiled=True)

    def feed(part, one, two, g_gate, g_up):
        lines = pl.BlockSpec((16, 4, 8, 128), lambda i: (0, i, 0, 0))
        return tiled_call(
            feed_kernel,
            [
                shape(256, 2048, dtype=BF16),
                shape(TOK, D + 384, dtype=BF16),
                shape(TOK, D + 384, dtype=BF16),
                shape(16, 16, 8, 128),
                shape(16, 16, 8, 128),
            ],
            [one, two, d_act, pick4, mlp_set, mlp_set, gu_out, gu_out, mlp_set, mlp_set, g_gate, g_up],
            [
                once(TOK, D),
                once(TOK, D),
                pl.BlockSpec((256, 512), lambda i: (part, i)),
                pl.BlockSpec((256, 128), lambda i: (part, 0)),
                pl.BlockSpec((D, 512), lambda i: (0, i)),
                pl.BlockSpec((D, 512), lambda i: (0, i + 4)),
                pl.BlockSpec((128, 512), lambda i: (0, i)),
                pl.BlockSpec((128, 512), lambda i: (0, i + 4)),
                block(D, 256, 24),
                pl.BlockSpec((512, 128), lambda i: (i, 50)),
                lines,
                lines,
            ],
            [pl.BlockSpec((256, 512), lambda i: (0, i))]
            + [whole_spec(TOK, D + 384)] * 2
            + [lines] * 2,
            [pltpu.VMEM((D + 384, 256), F32), pltpu.VMEM((256, 256), BF16), pltpu.VMEM((256, D), BF16)],
            flops=2 * 256 * 4096 * D * 2,
            vmem=52,
        )

    none = jnp.zeros((16, 16, 8, 128), F32)
    act_a, back_1, back_3, g_gate, g_up = feed(0, n1, n3, none, none)
    act_b, back_b, back_2, g_gate, g_up = feed(1, normed_mlp, n2, g_gate, g_up)
    back = [along_x(back_1, 3), along_x(back_3, 1), back_b, along_x(back_2, 2)]

    gu_lines = 2.0 * jnp.concatenate([g_gate, g_up], axis=1).reshape(16, 256, 128)
    gu_lines = a2a(gu_lines.astype(BF16), NATURAL)
    *down, g_down_in = tiled_call(
        down_kernel,
        [shape(TOK, D, dtype=BF16)] * 4 + [shape(2048, 128, dtype=BF16)],
        [act_a, act_b, d_small_down, mlp_set],
        [
            pl.BlockSpec((256, 512), lambda i: (0, i)),
            pl.BlockSpec((256, 512), lambda i: (0, i)),
            once(512, 128),
            pl.BlockSpec((512, D), lambda i: (i, 2)),
        ],
        [whole_spec(TOK, D)] * 4 + [pl.BlockSpec((512, 128), lambda i: (i, 0))],
        [pltpu.VMEM((512, D), F32)],
        flops=2 * 512 * 2048 * D,
        deps=[back_b, back[0], back[1]],
        vmem=52,
    )
    d_hidden, d_attn, d_small_gu, small_down = call(
        d_hidden_kernel,
        [
            shape(TOK, D),
            shape(TOK, D, dtype=BF16),
            shape(TOK, 256, dtype=BF16),
            shape(TOK, 128, dtype=BF16),
        ],
        [hidden, cot_own, gain_mlp, *back, mlp_set, pick_f],
        deps=[down[0], gu_lines],
        specs=[None] * 7 + [block(D, 256, 24), None],
        vmem=52,
    )

    mine, theirs, d_small_o, halves = call(
        project_back_kernel,
        [
            shape(256, 1024),
            shape(256, 1024, dtype=BF16),
            shape(256, 128, dtype=BF16),
            shape(256, 1024, dtype=BF16),
        ],
        [place, d_attn, other_core(d_attn), o_whole, o_whole, out_out, pick_f],
        specs=[SMEM, None, None, o_spec, oa_spec, None, None],
        flops=2 * 256 * D * 1024,
        vmem=20,
    )
    (send,) = call(
        pack_kernel, [shape(16, TOK, 128, dtype=BF16)], [mine, other_core(theirs)], vmem=6
    )

    down = [
        along_x(down[0], 3),
        along_x(down[1], 1),
        down[2],
        along_x(down[3], 2),
    ]
    d_out = a2a(send, BLOCKS).reshape(GTOK, 128)
    (early,) = call(
        early_grads_kernel,
        [shape(16, 384, 128, dtype=BF16)],
        [
            g_down_in,
            d_small_gu,
            normed_mlp,
            small_down,
            cot_own,
            d_small_o,
            attended,
            small_o,
            halves,
            fold,
        ],
        scratch=[pltpu.VMEM((16, 384, 128), F32)],
        deps=[d_out],
        vmem=28,
    )
    early = a2a(early, NATURAL)
    q_out, k_out, v_out = call(
        unpack_qkv_kernel,
        [shape(128, 1024, dtype=BF16), shape(128, 512, dtype=BF16), shape(128, 512, dtype=BF16)],
        [t2[:, 1536:]],
        scratch=[pltpu.VMEM((D, 128), F32)],
        vmem=8,
    )
    (dz,) = call(
        attend_back_kernel,
        [shape(GTOK, 256, dtype=BF16)],
        [z, d_out, stat],
        deps=[q_out],
        scratch=[pltpu.VMEM((GTOK, HDIM), F32), pltpu.VMEM((GTOK, HDIM), F32)],
        flops=5 * 2 * 2 * 30 * CLEN * CLEN * HDIM * 4,
        vmem=24,
    )
    parts = a2a(dz.reshape(16, TOK, 256), BLOCKS)
    plane, g_down_in = call(
        sums_kernel,
        [shape(8, 120, 128), shape(128, 128)],
        [source_slot, gu_lines, early],
        deps=[dz],
        scratch=[pltpu.VMEM((512, 128), F32), pltpu.VMEM((256, 128), F32)],
        specs=[SMEM, None, None],
        vmem=14,
    )
    def in_chip(v):
        v = v.reshape(4, 2, *v.shape[1:])

        def to_chip(k):
            return lax.dynamic_index_in_dim(v, (x + k) % 4, 0, keepdims=False)

        by_chip = jnp.stack([to_chip(0)] + [along_x(to_chip(k), k) for k in (1, 2, 3)])
        keep = lax.dynamic_index_in_dim(by_chip, c, 1, keepdims=False)
        return keep, other_core(lax.dynamic_index_in_dim(by_chip, 1 - c, 1, keepdims=False))

    keep, take = in_chip(plane)
    (output,) = call(
        output_kernel,
        [shape(TOK, D, dtype=BF16)],
        [hidden, *down, down_out, small_down],
        deps=[take],
        vmem=12,
    )
    output = swap_mid(output)
    d_joint, mine_small, their_small = call(
        qkv_back_kernel,
        [shape(256, 1536, dtype=BF16), shape(TOK, 384), shape(TOK, 384, dtype=BF16)],
        [parts, q_out, k_out, v_out, cq, sq, ckv, skv],
        deps=[take],
        vmem=12,
    )
    d_small_qkv, late = call(
        late_grads_kernel,
        [shape(TOK, 384, dtype=BF16), shape(D, 256, dtype=BF16)],
        [mine_small, other_core(their_small), pick_f, normed_attn, small_qkv, d_joint, fold],
        scratch=[pltpu.VMEM((D, 128), F32)],
        vmem=14,
    )
    mine, theirs = call(
        d_normed_kernel,
        [shape(TOK, D), shape(TOK, D, dtype=BF16)],
        [d_joint, t2],
        deps=[late],
        specs=[None, w_spec],
        flops=2 * 256 * D * 1536,
        vmem=20,
    )
    late = a2a(late.reshape(128, 16, 256), NATURAL + PLANE)
    (input_grad,) = call(
        last_kernel,
        [shape(TOK, D, dtype=BF16)],
        [x_own, d_hidden, gain_attn, mine, other_core(theirs), d_small_qkv, heads],
        specs=[None] * 6 + [block(D, 384, 1)],
        vmem=14,
    )
    input_grad = swap_mid(input_grad)

    late_first, late_second = call(
        late_sums_kernel,
        [shape(8, 16, 128), shape(2, 16, 128)],
        [device_slot, late],
        specs=[SMEM, None],
        vmem=8,
    )
    both = keep + take
    gu = both[:, :32]
    gu = [lax.dynamic_index_in_dim(gu, (x - k) % 4, 0, keepdims=False) for k in range(4)]
    gu = jnp.stack(gu).reshape(4, 2, 2, 2, 4, 128).transpose(1, 3, 2, 4, 0, 5)
    grad_gu_out = gu.reshape(1, 2 * UNITS)
    half = g_down_in.reshape(2, 64, 128)
    to_other = lax.dynamic_index_in_dim(half, 1 - c, 0, keepdims=False)
    grad_down_in = lax.dynamic_index_in_dim(half, c, 0, keepdims=False)
    grad_down_in = swap_mid(grad_down_in + other_core(to_other))
    total = jnp.sum(both[:, 32:112], axis=0)
    first = total[:64].reshape(4, 16, 2, 4, RANK).transpose(1, 3, 0, 2, 4).reshape(16, 4, 128)
    grad_gu_in = swap_mid(first[:, :2]).reshape(16, 256)
    grad_out_in = swap_mid(first[:, 2])
    grad_down_out = swap_mid(total[64:80].reshape(1, D))
    keep, take = jnp.sum(keep[:, 112:], axis=0), jnp.sum(take[:, 112:], axis=0)
    halves = jnp.where(c == 0, jnp.stack([keep, take]), jnp.stack([take, keep]))
    grad_out_out = swap_mid(halves.reshape(1, D))
    first = late_first[:, :, :48].reshape(8, 16, 3, RANK).transpose(1, 2, 0, 3)
    grad_qkv_in = swap_mid(first.reshape(16, 3, 128)).reshape(16, 384)
    grad_q_out = swap_mid(late_second[:, :8].reshape(1, D))
    kv = late_second[:, 8:12].reshape(2, 4, 2, HDIM).transpose(2, 0, 1, 3).reshape(2, 512)
    grad_kv_out = swap_mid(kv).reshape(1, 1024)

    return (
        output[None],
        input_grad[None],
        grad_qkv_in,
        grad_q_out,
        grad_kv_out,
        grad_out_in,
        grad_out_out,
        grad_gu_in,
        grad_gu_out,
        grad_down_in,
        grad_down_out,
    )


def solution(mesh):
    fine = Mesh(mesh.devices.reshape(2, 2, 4, 4, 2), AXES)
    tok = P(PLANE, BLOCKS, None)
    flat = P(AXES)
    rows = P(AXES, None)
    return jax.shard_map(
        local,
        mesh=fine,
        in_specs=(tok, P(PLANE, None), flat, flat) + (rows,) * 13 + (tok,),
        out_specs=(tok, tok) + (rows,) * 9,
        check_vma=False,
    )
```

```python
import functools

import jax
import jax.numpy as jnp
from jax import lax
from jax.experimental import pallas as pl
from jax.experimental.pallas import tpu as pltpu
from jax.sharding import Mesh
from jax.sharding import PartitionSpec as P

HEADS = 32
KVH = 8
HDIM = 64
D = HEADS * HDIM
UNITS = 8192
PROMPT = 1024
CLEN = 256
GTOK = 2048
TOK = 128
RANK = 16

EPS = 1e-5
SKIP = 0.22
ROPE_BASE = 10000000.0
NEG = -1e30

F32 = jnp.float32
BF16 = jnp.bfloat16

AXES = ("zl", "zh", "y", "x", "c")
BLOCKS = ("zl", "zh", "y")
NATURAL = ("zh", "zl", "y")
PLANE = ("x", "c")

def mm(a, b):
    return jnp.dot(a, b, preferred_element_type=F32)


def mm_nt(a, b):
    return lax.dot_general(a, b, (((1,), (1,)), ((), ())), preferred_element_type=F32)


def mm_tn(a, b):
    return lax.dot_general(a, b, (((0,), (0,)), ((), ())), preferred_element_type=F32)


def swap_mid(v, axis=-1):
    axis = axis % v.ndim
    n = v.shape[axis] // 4
    q = [lax.slice_in_dim(v, k * n, (k + 1) * n, axis=axis) for k in (0, 2, 1, 3)]
    return jnp.concatenate(q, axis=axis)


def a2a(v, axes):
    return lax.all_to_all(v, axes, 0, 0, tiled=True)


def other_core(v):
    return lax.ppermute(v, "c", [(0, 1), (1, 0)])


def along_x(v, k):
    return lax.ppermute(v, "x", [(i, (i + k) % 4) for i in range(4)])


MIB = 1024 * 1024


def nbytes(arrays):
    return sum(a.size * a.dtype.itemsize for a in arrays)


def job(g, j):
    return (j // 2) * 4 + g * 2 + j % 2


def far_of(one, three):
    half = one.shape[0] // 2
    return jnp.concatenate([along_x(one[:half], 1), along_x(three[half:], 3)])


def from_x(v):
    one, three = along_x(v, 1), along_x(v, 3)
    return one, three, far_of(one, three)


def call(kernel, outs, args, scratch=(), specs=None, flops=0, vmem=24, deps=()):
    if specs is None:
        specs = [None] * len(args)
    ins = [pl.BlockSpec(memory_space=pltpu.VMEM) if s is None else s for s in specs]
    ins = ins + [pl.BlockSpec(memory_space=pl.ANY)] * len(deps)
    return pl.pallas_call(
        ignoring(kernel, len(args), len(deps)),
        name=kernel.__name__,
        grid=(1,),
        out_shape=outs,
        in_specs=ins,
        out_specs=[pl.BlockSpec(memory_space=pltpu.VMEM)] * len(outs),
        scratch_shapes=list(scratch),
        compiler_params=pltpu.CompilerParams(vmem_limit_bytes=vmem * MIB),
        cost_estimate=pl.CostEstimate(
            flops=flops, bytes_accessed=nbytes(args) + nbytes(outs), transcendentals=0
        ),
    )(*args, *deps)


def tiled_call(
    kernel, outs, args, specs, out_specs, scratch=(), flops=0, steps=4, vmem=32, deps=()
):
    size = nbytes(outs) + 2 * flops // 1024
    return pl.pallas_call(
        ignoring(kernel, len(args), len(deps)),
        name=kernel.__name__,
        grid=(steps,),
        out_shape=outs,
        in_specs=specs + [pl.BlockSpec(memory_space=pl.ANY)] * len(deps),
        out_specs=out_specs,
        scratch_shapes=list(scratch),
        compiler_params=pltpu.CompilerParams(vmem_limit_bytes=vmem * MIB),
        cost_estimate=pl.CostEstimate(flops=flops, bytes_accessed=size, transcendentals=0),
    )(*args, *deps)


def shape(*dims, dtype=F32):
    return jax.ShapeDtypeStruct(dims, dtype)


def block(rows, cols, index):
    return pl.BlockSpec((rows, cols), lambda i: (0, index), pipeline_mode=pl.Buffered(1))


def once(rows, cols):
    return pl.BlockSpec((rows, cols), lambda i: (0, 0), pipeline_mode=pl.Buffered(1))


def whole_spec(rows, cols):
    return pl.BlockSpec((rows, cols), lambda i: (0, 0))


def ignoring(kernel, first, count):
    def body(*refs):
        kernel(*refs[:first], *refs[first + count :])

    return body


def gate(v, *deps):
    def copy(ref, out):
        out[...] = ref[...]

    return call(copy, [jax.ShapeDtypeStruct(v.shape, v.dtype)], [v], deps=deps, vmem=8)[0]


def segment_of(block_index):
    return jnp.where(block_index < 8, 0, 1 + (block_index - 8) // 2)


SMEM = pl.BlockSpec(memory_space=pltpu.SMEM)


def rope(t, cos, sin):
    lane = lax.broadcasted_iota(jnp.int32, t.shape, 1) % HDIM
    partner = jnp.where(lane < HDIM // 2, pltpu.roll(t, 96, 1), pltpu.roll(t, 32, 1))
    return t * cos + partner * sin


def assemble(x, pieces, whole):
    for piece, ahead in zip(pieces, (0, 3, 1, 2)):
        at = lax.rem(x + ahead, 4) * 32

        def place(i, _, piece=piece, at=at):
            to = pl.multiple_of(i * 128 + at, 32)
            whole[pl.ds(to, 32), :] = piece[pl.ds(pl.multiple_of(i * 32, 32), 32), :]
            return 0

        lax.fori_loop(0, 16, place, 0)


def gain_row(g, first):
    lane = lax.broadcasted_iota(jnp.int32, (128, 128), 1)
    row = lax.broadcasted_iota(jnp.int32, (128, 128), 0)
    tiled = mm(g.astype(BF16), (row == first + lane % 16).astype(BF16))
    tiled = jnp.where(lane // 16 == row % 8, tiled, 0.0).astype(BF16)
    to_row = lax.broadcasted_iota(jnp.int32, (16, 128), 1) // 8
    to_row = (to_row == lax.broadcasted_iota(jnp.int32, (16, 128), 0)).astype(BF16)
    rows = mm(to_row, tiled)
    return jnp.concatenate([rows[k : k + 1] for k in range(16)], axis=1)


def only_keys(kv):
    lane = lax.broadcasted_iota(jnp.int32, kv.shape, 1) % 128
    return jnp.where(lane < HDIM, kv, 0.0).astype(BF16), jnp.where(lane < HDIM, 0.0, kv).astype(BF16)


def qkv_kernel(
    place, x, e, pick, cq, sq, ckv, skv, send, normed, small, gain, gain_mlp, n, s_all, wide
):
    core = place[1]
    wide[...] = e[:, 768:896].astype(F32)
    q_out = jnp.concatenate([wide[pl.ds(t, 128, stride=16), :] for t in range(2)], axis=1)
    q_out = q_out.astype(BF16)
    k_out, v_out = only_keys(wide[pl.ds(2, 128, stride=16), :])
    gain[...] = gain_row(wide[pl.ds(3, 128, stride=16), :], 0)
    gain_mlp[...] = gain_row(wide[pl.ds(3, 128, stride=16), :], 16)
    for k in range(4):
        rows = slice(2 * k * TOK, (2 * k + 2) * TOK)
        v = x[rows, :].astype(F32)
        r = lax.rsqrt(jnp.mean(v * v, axis=1, keepdims=True) + EPS)
        n[rows, :] = (v * r * gain[...]).astype(BF16)
        s = mm(n[rows, :], e[:, 384:768]).astype(BF16)
        s = jnp.concatenate(
            [s[:TOK] * pick[2 * k : 2 * k + 1, :], s[TOK:] * pick[2 * k + 1 : 2 * k + 2, :]], axis=0
        )
        s_all[rows, :] = s
        q = mm(n[rows, :], e[:, :256]) + 2.0 * mm(s[:, :128], q_out)
        kv = mm(n[rows, :], e[:, 256:384]) + 2.0 * (
            mm(s[:, 128:256], k_out) + mm(s[:, 256:], v_out)
        )
        for o in range(2):
            here = slice(o * TOK, (o + 1) * TOK)
            t = rope(kv[here], ckv[...], skv[...]).astype(BF16)
            at = k * 4 + 2 * lax.rem(core + o, 2)
            for j in range(2):
                p = rope(q[here, j * 128 : (j + 1) * 128], cq[...], sq[...]).astype(BF16)
                send[at + j, :, 0:128] = p
                send[at + j, :, 128:256] = t
    own = pl.multiple_of((2 * place[0] + core) * TOK, TOK)
    other = pl.multiple_of((2 * place[0] + 1 - core) * TOK, TOK)
    normed[...] = n[pl.ds(own, TOK), :]
    small[:TOK, :] = s_all[pl.ds(own, TOK), :]
    small[TOK:, :] = s_all[pl.ds(other, TOK), :]


def heads_of(ref, rows, scale=None):
    t = ref[rows, :128]
    both = jnp.concatenate([t[:, :HDIM], t[:, HDIM:]], axis=0)
    return both if scale is None else both * jnp.asarray(scale, BF16)


def allowed_in_block():
    key = lax.broadcasted_iota(jnp.int32, (CLEN, 2 * CLEN), 0)
    query = lax.broadcasted_iota(jnp.int32, (CLEN, 2 * CLEN), 1) % CLEN
    return key <= query


def attend_kernel(z, out, stat):
    allowed = allowed_in_block()
    for i in range(GTOK // CLEN):
        rows = slice(i * CLEN, (i + 1) * CLEN)
        full = min(i, PROMPT // CLEN) * CLEN
        q = heads_of(z, rows, 1.0 / 64.0)
        sd = jnp.where(allowed, mm_nt(z[rows, 128:192], q), NEG)
        top = jnp.max(sd, axis=0, keepdims=True)
        if full:
            sf = mm_nt(z[0:full, 128:192], q)
            top = jnp.maximum(top, jnp.max(sf, axis=0, keepdims=True))
        pd = jnp.exp(sd - top)
        total = jnp.sum(pd, axis=0, keepdims=True)
        o = mm_tn(z[rows, 192:256], pd.astype(BF16))
        if full:
            pf = jnp.exp(sf - top)
            total = total + jnp.sum(pf, axis=0, keepdims=True)
            o = o + mm_tn(z[0:full, 192:256], pf.astype(BF16))
        o = o / total
        stat[i : i + 1, :] = top + jnp.log(total)
        both = jnp.concatenate([o[:, :CLEN], o[:, CLEN:]], axis=0)
        out[rows, :] = both.T.astype(BF16)


def attend_back_kernel(z, d_out, stat, dz, dk, dv):
    allowed = allowed_in_block()
    dk[...] = jnp.zeros_like(dk)
    dv[...] = jnp.zeros_like(dv)
    for i in range(GTOK // CLEN):
        rows = slice(i * CLEN, (i + 1) * CLEN)
        full = min(i, PROMPT // CLEN) * CLEN
        q = heads_of(z, rows, 1.0 / 64.0)
        do = heads_of(d_out, rows)
        lse = stat[i : i + 1, :]
        kd = z[rows, 128:192]
        pd = jnp.exp(jnp.where(allowed, mm_nt(kd, q), NEG) - lse)
        dpd = mm_nt(z[rows, 192:256], do)
        inner = jnp.sum(pd * dpd, axis=0, keepdims=True)
        if full:
            kf = z[0:full, 128:192]
            pf = jnp.exp(mm_nt(kf, q) - lse)
            dpf = mm_nt(z[0:full, 192:256], do)
            inner = inner + jnp.sum(pf * dpf, axis=0, keepdims=True)
        dsd = (pd * (dpd - inner)).astype(BF16)
        dq = mm_tn(kd, dsd)
        dk[rows, :] += mm(dsd, q)
        dv[rows, :] += mm(pd.astype(BF16), do)
        if full:
            dsf = (pf * (dpf - inner)).astype(BF16)
            dq = dq + mm_tn(kf, dsf)
            dk[0:full, :] += mm(dsf, q)
            dv[0:full, :] += mm(pf.astype(BF16), do)
        dq = dq * (1.0 / 64.0)
        both = jnp.concatenate([dq[:, :CLEN], dq[:, CLEN:]], axis=0)
        dz[rows, 0:128] = both.T.astype(BF16)
    dz[:, 128:256] = jnp.concatenate([dk[...], dv[...]], axis=1).astype(BF16)


def project_kernel(
    place, mine, theirs, e0, e1, e2, e3, pick,
    part, their_part, small, attended, whole, a_out, att, wide,
):
    assemble(place[0], (e0, e1, e2, e3), whole)
    wide[...] = whole[:, 1152:1280].astype(F32)
    for t in range(16):
        a_out[:, t * 128 : (t + 1) * 128] = wide[pl.ds(t, 128, stride=16), :].astype(BF16)
    c = place[1]
    here = pl.multiple_of(c * 1024, 1024)
    there = pl.multiple_of((1 - c) * 1024, 1024)
    for g in range(2):
        rows = slice(g * TOK, (g + 1) * TOK)
        for j in range(8):
            cols = slice(j * 128, (j + 1) * 128)
            att[0, rows, cols] = mine[job(g, j)]
            att[1, rows, cols] = theirs[job(1 - g, j)]
    m, t = att[0], att[1]
    attended[:, pl.ds(here, 1024)] = m[:TOK]
    attended[:, pl.ds(there, 1024)] = t[:TOK]
    s = mm(m, whole[pl.ds(here, 1024), 1024:1152]) + mm(t, whole[pl.ds(there, 1024), 1024:1152])
    s = s.astype(BF16)
    s = jnp.concatenate([s[:TOK] * pick[0:1, :128], s[TOK:] * pick[1:2, :128]], axis=0)
    small[...] = s
    both = (
        mm(m, whole[pl.ds(here, 1024), :1024])
        + mm(t, whole[pl.ds(there, 1024), :1024])
        + 2.0 * mm(s, a_out[:, pl.ds(here, 1024)])
    )
    part[...] = both[:TOK]
    their_part[...] = both[TOK:]


def hidden_kernel(place, x, mine, theirs, gain, hidden, normed):
    c = place[1]
    here = pl.multiple_of(c * 1024, 1024)
    there = pl.multiple_of((1 - c) * 1024, 1024)
    hidden[:, pl.ds(here, 1024)] = SKIP * mine[...]
    hidden[:, pl.ds(there, 1024)] = SKIP * theirs[...]
    h = x[...].astype(F32) + hidden[...]
    hidden[...] = h
    r = lax.rsqrt(jnp.mean(h * h, axis=1, keepdims=True) + EPS)
    normed[...] = (h * r * gain[...]).astype(BF16)


def halves_kernel(one, three, half_one, half_three):
    half_one[...] = one[: TOK // 2, :]
    half_three[...] = three[TOK // 2 :, :]


def unpack_kernel(outs, gu_out, down_out, wide):
    for k in range(3):
        wide[...] = outs[:, k * 128 : (k + 1) * 128].astype(F32)
        for t in range(16):
            at = (3 * t + k) * 128
            part = wide[pl.ds(t, 128, stride=16), :].astype(BF16)
            if at < 4096:
                gu_out[:, at : at + 128] = part
            else:
                down_out[:, at - 4096 : at - 3968] = part


def turn_kernel(cot, dm, turned):
    d = (SKIP * cot[...].astype(F32)).astype(BF16)
    dm[...] = d
    turned[...] = d.T


def d_act_kernel(dm, turned, a_out, a_in, pick, w, d_act, small):
    @pl.when(pl.program_id(0) == 0)
    def _():
        s = 2.0 * mm_nt(dm[...], a_out[...]) * pick[...].astype(F32)
        small[...] = s.astype(BF16)

    d_act[...] = mm(w[...], turned[...]).T + mm_nt(small[...], a_in[...])


def feed_kernel(
    n_one, n_two, d_act, pick, w_gate, w_up, o_gate, o_up, a_in, a_down, g_gate0, g_up0,
    act, back, back1, g_gate, g_up, total, small, turned, n,
):
    step = pl.program_id(0)

    @pl.when(step == 0)
    def _():
        n[:TOK, :] = n_one[...]
        n[TOK:, :] = n_two[...]
        s = mm(n[...], a_in[...]).astype(BF16)
        p = pick[...]
        s = s * jnp.concatenate([p, p], axis=1)
        small[...] = s
        turned[...] = s.T
        total[...] = jnp.zeros_like(total)

    x = n[...]
    gate = mm(x, w_gate[...]) + 2.0 * mm(small[:, :128], o_gate[...])
    up = mm(x, w_up[...]) + 2.0 * mm(small[:, 128:], o_up[...])
    sg = 1.0 / (1.0 + jnp.exp(-gate))
    gs = gate * sg
    act[...] = (gs * up).astype(BF16)
    da = d_act[...]
    dg = (da * up * (sg + gs * (1.0 - sg))).astype(BF16)
    du = (da * gs).astype(BF16)
    total[:D, :] += mm_nt(w_gate[...], dg) + mm_nt(w_up[...], du)
    total[D : D + 128, :] += mm_nt(o_gate[...], dg)
    total[D + 128 : D + 256, :] += mm_nt(o_up[...], du)
    total[D + 256 :, :] += mm_nt(a_down[...].T, act[...])
    for g0, out, d, rows in ((g_gate0, g_gate, dg, 0), (g_up0, g_up, du, 128)):
        g = mm(turned[rows : rows + 128, :], d)
        for t in range(4):
            out[:, t] = g0[:, t] + g[:, t * 128 : (t + 1) * 128].reshape(16, 8, 128)

    @pl.when(step == pl.num_programs(0) - 1)
    def _():
        back[...] = total[:, :TOK].T.astype(BF16)
        back1[...] = total[:, TOK:].T.astype(BF16)


def down_kernel(act_a, act_b, d_small, w, out, out1, out2, out3, g_in, total):
    step = pl.program_id(0)

    @pl.when(step == 0)
    def _():
        total[...] = jnp.zeros_like(total)

    for k, act in enumerate((act_a, act_b)):
        rows = slice(k * 256, (k + 1) * 256)
        total[rows, :] += mm(act[...], w[...])
    g = mm_tn(act_a[...], d_small[:256]) + mm_tn(act_b[...], d_small[256:])
    g_in[...] = g.astype(BF16)

    @pl.when(step == pl.num_programs(0) - 1)
    def _():
        for k, ref in enumerate((out, out1, out2, out3)):
            ref[...] = total[k * TOK : (k + 1) * TOK, :].astype(BF16)


def output_kernel(hidden, p0, p1, p2, p3, a_out, small, out):
    total = p0[...].astype(F32) + p1[...].astype(F32) + p2[...].astype(F32) + p3[...].astype(F32)
    out[...] = (hidden[...] + SKIP * (total + 2.0 * mm(small[...], a_out[...]))).astype(BF16)


def rms_back(v, gain, e):
    r = lax.rsqrt(jnp.mean(v * v, axis=1, keepdims=True) + EPS)
    we = gain * e
    return r * we - v * (r * r * r) * jnp.mean(v * we, axis=1, keepdims=True)


def d_hidden_kernel(
    hidden, cot, gain, p0, p1, p2, p3, a_in, pick, d_hidden, d_attn, small, small_down
):
    total = p0[...].astype(F32) + p1[...].astype(F32) + p2[...].astype(F32) + p3[...].astype(F32)
    s = (2.0 * total[:, D : D + 256] * pick[0:1, :256]).astype(BF16)
    small[...] = s
    small_down[...] = (total[:, D + 256 :] * pick[0:1, :128]).astype(BF16)
    e = total[:, :D] + mm_nt(s, a_in[...])
    d = cot[...].astype(F32) + rms_back(hidden[...], gain[...], e)
    d_hidden[...] = d
    d_attn[...] = (SKIP * d).astype(BF16)


def project_back_kernel(place, own, other, w, a_in, a_out, pick, mine, theirs, small, halves):
    c = place[1]
    here = pl.multiple_of(c * 1024, 1024)
    there = pl.multiple_of((1 - c) * 1024, 1024)
    full = jnp.concatenate([own[...], other[...]], axis=0)
    s = 2.0 * mm_nt(full, a_out[...])
    s = jnp.concatenate([s[:TOK] * pick[0:1, :128], s[TOK:] * pick[1:2, :128]], axis=0)
    s = s.astype(BF16)
    small[...] = s
    half = jnp.concatenate([own[:, pl.ds(here, 1024)], other[:, pl.ds(here, 1024)]], axis=0)
    halves[...] = half
    theirs[...] = mm_nt(half, w[pl.ds(there, 1024), :]).astype(BF16)
    mine[...] = mm_nt(half, w[pl.ds(here, 1024), :]) + mm_nt(s, a_in[pl.ds(here, 1024), :])


def pack_kernel(mine, theirs, send):
    for g in range(2):
        rows = slice(g * TOK, (g + 1) * TOK)
        swapped = slice((1 - g) * TOK, (2 - g) * TOK)
        for j in range(8):
            cols = slice(j * 128, (j + 1) * 128)
            send[job(g, j)] = (mine[rows, cols] + theirs[swapped, cols].astype(F32)).astype(BF16)


def early_grads_kernel(
    g_down_in, d_small_gu, normed, small_down, cot, d_small_o, attended, small_o, halves, fold,
    out, lines,
):
    f = mm(d_small_gu[...], fold[:256, :]).astype(BF16)[:, :HDIM]
    g = mm_tn(f, normed[...])
    f = mm(d_small_o[:TOK], fold[256:384, :]).astype(BF16)[:, :HDIM]
    g = g + mm_tn(f, attended[...])
    dm = (SKIP * cot[...].astype(F32)).astype(BF16)
    g_down = 2.0 * mm_tn(small_down[...], dm)
    g_o = 2.0 * mm_tn(small_o[...], halves[...])
    for k in range(16):
        lines[k, 128:192, :] = g[:, k * 128 : (k + 1) * 128]
        rows = slice(k * 8, (k + 1) * 8)
        for t in range(16):
            lines[k, 192 + t * 8 : 200 + t * 8, :] = g_down[rows, t * 128 : (t + 1) * 128]
        for t in range(8):
            lines[k, 320 + t * 8 : 328 + t * 8, :] = g_o[rows, t * 128 : (t + 1) * 128]
        out[k, :128, :] = g_down_in[k * 128 : (k + 1) * 128, :]
        out[k, 128:, :] = lines[k, 128:, :].astype(BF16)


def sums_kernel(slot, gu, early, plane, g_down_in, first, total):
    first[...] = jnp.zeros_like(first)
    total[...] = gu[0].astype(F32)
    for k in range(1, 16):
        total[...] += gu[k].astype(F32)
    for r in range(8):
        plane[r, 0:32, :] = total[pl.ds(r, 32, stride=8), :]
    d = early[0, :128, :].astype(F32)
    o = early[0, 192:384, :].astype(F32)
    for k in range(16):
        at = pl.multiple_of(slot[k] * HDIM, HDIM)
        first[pl.ds(at, HDIM), :] += early[k, 128:192, :].astype(F32)
        if k:
            d = d + early[k, :128, :].astype(F32)
            o = o + early[k, 192:384, :].astype(F32)
    g_down_in[...] = d
    total[:192, :] = o
    turned = first[...].T
    for r in range(8):
        for k in range(4):
            part = turned[r * 16 : (r + 1) * 16, k * 128 : (k + 1) * 128]
            plane[r, 32 + k * 16 : 48 + k * 16, :] = part
        plane[r, 96:120, :] = total[pl.ds(r, 24, stride=8), :]


def unpack_qkv_kernel(outs, q_out, k_out, v_out, wide):
    wide[...] = outs[...].astype(F32)
    q = [wide[pl.ds(t, 128, stride=16), :] for t in range(8)]
    q_out[...] = jnp.concatenate(q, axis=1).astype(BF16)
    kv = [wide[pl.ds(8 + t, 128, stride=16), :] for t in range(4)]
    k_out[...], v_out[...] = only_keys(jnp.concatenate(kv, axis=1))


def qkv_back_kernel(
    parts, q_out, k_out, v_out, cq, sq, ckv, skv, d_joint, mine_small, their_small
):
    for g in range(2):
        rows = slice(g * TOK, (g + 1) * TOK)
        for j in range(8):
            t = parts[job(g, j), :, 0:128].astype(F32)
            d_joint[rows, j * 128 : (j + 1) * 128] = rope(t, cq[...], -sq[...]).astype(BF16)
        for j in range(4):
            t = parts[job(g, 2 * j), :, 128:256].astype(F32)
            t = t + parts[job(g, 2 * j + 1), :, 128:256].astype(F32)
            d_joint[rows, 1024 + j * 128 : 1024 + (j + 1) * 128] = rope(
                t, ckv[...], -skv[...]
            ).astype(BF16)
    dq, dkv = d_joint[:, :1024], d_joint[:, 1024:]
    small = 2.0 * jnp.concatenate(
        [mm_nt(dq, q_out[...]), mm_nt(dkv, k_out[...]), mm_nt(dkv, v_out[...])], axis=1
    )
    mine_small[...] = small[:TOK]
    their_small[...] = small[TOK:].astype(BF16)


def late_grads_kernel(
    mine_small, their_small, pick, normed, small_qkv, d_joint, fold, small, out, g
):
    s = ((mine_small[...] + their_small[...].astype(F32)) * pick[0:1, :]).astype(BF16)
    small[...] = s
    f = mm(s, fold[...]).astype(BF16)
    out[:, :128] = mm_tn(normed[...], f).astype(BF16)
    gq = 2.0 * mm_tn(small_qkv[:, :128], d_joint[:, :1024])
    gk = mm_tn(small_qkv[:, 128:256], d_joint[:, 1024:])
    gv = mm_tn(small_qkv[:, 256:], d_joint[:, 1024:])
    lane = lax.broadcasted_iota(jnp.int32, gk.shape, 1) % 128
    gkv = 2.0 * jnp.where(lane < HDIM, gk, gv)
    for t in range(8):
        g[pl.ds(t, 128, stride=16), :] = gq[:, t * 128 : (t + 1) * 128]
    for t in range(4):
        g[pl.ds(8 + t, 128, stride=16), :] = gkv[:, t * 128 : (t + 1) * 128]
        g[pl.ds(12 + t, 128, stride=16), :] = jnp.zeros((128, 128), F32)
    out[:, 128:] = g[...].astype(BF16)


def late_sums_kernel(slot, late, first, second):
    first[...] = jnp.zeros_like(first)
    second[...] = jnp.zeros_like(second)

    def add(k, _):
        for core in range(2):
            v = late[2 * k + core].astype(F32)
            at = slot[2 * k + core]
            first[at] += v[:, :128]
            second[core] += v[:, 128:]
        return 0

    lax.fori_loop(0, 64, add, 0)


def d_normed_kernel(d_joint, w, mine, theirs):
    dn = mm_nt(d_joint[...], w[...])
    mine[...] = dn[:TOK]
    theirs[...] = dn[TOK:].astype(BF16)


def last_kernel(x, d_hidden, gain, mine, theirs, small, a, grad):
    dn = mine[...] + theirs[...].astype(F32) + mm_nt(small[...], a[...])
    v = x[...].astype(F32)
    grad[...] = (d_hidden[...] + rms_back(v, gain[...], dn)).astype(BF16)


def local(
    tokens,
    adapter_ids,
    norm_gain_attn,
    norm_gain_mlp,
    qkv_weight,
    output_projection_weight,
    gate_up_weight,
    down_projection_weight,
    qkv_adapter_in,
    q_adapter_out,
    kv_adapter_out,
    out_adapter_in,
    out_adapter_out,
    gate_up_adapter_in,
    gate_up_adapter_out,
    down_adapter_in,
    down_adapter_out,
    cotangent,
):
    c = lax.axis_index("c")
    x = lax.axis_index("x")
    b = lax.axis_index(BLOCKS)
    place = jnp.stack([x, c]).astype(jnp.int32)

    x_own = swap_mid(tokens[0])
    cot_own = swap_mid(cotangent[0])
    x_plane = lax.all_gather(x_own, PLANE, axis=0, tiled=True)

    q_w = swap_mid(qkv_weight[:, :D])
    k_w = swap_mid(qkv_weight[:, D : D + 512]).reshape(16, 8, 1, HDIM)
    v_w = swap_mid(qkv_weight[:, D + 512 :]).reshape(16, 8, 1, HDIM)
    kv_w = jnp.concatenate([k_w, v_w], axis=2).reshape(16, 1024)
    a_in = swap_mid(qkv_adapter_in.reshape(16, 3, 128)).reshape(16, 384)
    qo = swap_mid(q_adapter_out)
    ko = swap_mid(kv_adapter_out[:, :512]).reshape(8, 1, HDIM)
    vo = swap_mid(kv_adapter_out[:, 512:]).reshape(8, 1, HDIM)
    kvo = jnp.concatenate([ko, vo], axis=1).reshape(1, 1024)
    ids = adapter_ids[0]
    extra = jnp.concatenate([norm_gain_attn, norm_gain_mlp, ids.astype(BF16), jnp.zeros(91, BF16)])
    outs = jnp.concatenate(
        [
            qo.reshape(8, 2, 128),
            kvo.reshape(8, 1, 128),
            jnp.broadcast_to(extra, (8, 1, 128)),
            jnp.zeros((8, 12, 128), BF16),
        ],
        axis=1,
    )
    payload = jnp.concatenate(
        [
            q_w.reshape(16, 8, 256).transpose(1, 0, 2),
            kv_w.reshape(16, 8, 128).transpose(1, 0, 2),
            jnp.broadcast_to(a_in, (8, 16, 384)),
            outs,
        ],
        axis=2,
    )
    heads = payload.reshape(2, 4, 16, 896).transpose(1, 0, 2, 3).reshape(8, 16, 896)
    in_plane = a2a(heads, PLANE)
    ids_all = in_plane[:, 3, 800:805].astype(F32)
    heads = jnp.broadcast_to(in_plane.reshape(1, 128, 896), (16, 128, 896))
    heads = a2a(heads, NATURAL).reshape(D, 896)

    o_w = swap_mid(output_projection_weight).reshape(16, 2, 1024)
    o_out = swap_mid(out_adapter_out).reshape(16, 128)
    payload = jnp.concatenate(
        [
            o_w.transpose(1, 0, 2),
            jnp.broadcast_to(swap_mid(out_adapter_in), (2, 16, 128)),
            jnp.broadcast_to(o_out, (2, 16, 128)),
        ],
        axis=2,
    )

    def chip_rows(v):
        keep = lax.dynamic_index_in_dim(v, c, 0, keepdims=False)
        take = other_core(lax.dynamic_index_in_dim(v, 1 - c, 0, keepdims=False))
        return jnp.where(c == 0, jnp.concatenate([keep, take]), jnp.concatenate([take, keep]))

    chip = chip_rows(payload)
    o_mine = lax.all_gather(gate(chip, x_plane, in_plane), NATURAL, axis=0, tiled=True)
    o_set = [o_mine, *from_x(o_mine)]

    gu = gate_up_weight.reshape(16, 2, 2, 2, 4, 4, 128).transpose(5, 0, 1, 3, 2, 4, 6)
    gu = gu.reshape(4, 16, 4096)
    guo = gate_up_adapter_out.reshape(2, 2, 2, 4, 4, 128).transpose(4, 0, 2, 1, 3, 5)
    guo = guo.reshape(4, 4096)
    outs = jnp.concatenate([guo, jnp.broadcast_to(swap_mid(down_adapter_out), (4, D))], axis=1)
    gu_in = swap_mid(gate_up_adapter_in.reshape(16, 2, 128)).reshape(16, 256)
    to_x = jnp.concatenate(
        [
            gu,
            jnp.broadcast_to(gu_in, (4, 16, 256)),
            outs.reshape(4, 16, 384),
        ],
        axis=2,
    )

    to_x = gate(to_x, x_plane)

    def for_chip(k):
        return lax.dynamic_index_in_dim(to_x, (x + k) % 4, 0, keepdims=False)

    by_chip = [for_chip(0)] + [along_x(for_chip(k), k) for k in (1, 2, 3)]
    by_chip = jnp.stack(by_chip)

    def of_pair(core):
        two = [
            lax.dynamic_index_in_dim(by_chip, (x - 2 * core - j) % 4, 0, keepdims=False)
            for j in range(2)
        ]
        return jnp.stack(two)

    keep = of_pair(c)
    take = other_core(of_pair(1 - c))
    rows = jnp.where(c == 0, jnp.stack([keep, take], 1), jnp.stack([take, keep], 1))
    plane = rows.reshape(64, 4736)
    down_w = swap_mid(down_projection_weight)
    down_in = swap_mid(down_adapter_in)
    plane = jnp.concatenate(
        [plane[:, :4096], down_w, plane[:, 4096:4352], down_in, plane[:, 4352:]], axis=1
    )


    segment = segment_of(b)
    start = jnp.where(b < 8, b * TOK, PROMPT + ((b - 8) % 2) * TOK)
    positions = start + jnp.arange(TOK, dtype=jnp.int32)
    frequency = ROPE_BASE ** (-(jnp.arange(HDIM // 2, dtype=F32) * 2.0) / HDIM)
    angles = positions.astype(F32)[:, None] * frequency[None, :]
    cos, sin = jnp.cos(angles), jnp.sin(angles)
    one, zero = jnp.ones((TOK, HDIM), F32), jnp.zeros((TOK, HDIM), F32)
    cq = jnp.concatenate([cos] * 4, axis=1)
    sq = jnp.concatenate([-sin, sin, -sin, sin], axis=1)
    ckv = jnp.concatenate([cos, cos, one], axis=1)
    skv = jnp.concatenate([-sin, sin, zero], axis=1)

    col = jnp.arange(128)
    col_adapter = ((col >> 5) & 1) * 4 + ((col >> 6) & 1) * 2 + ((col >> 4) & 1)
    here = (jnp.arange(5) == segment).astype(F32)

    def picks(adapters):
        a = jnp.sum(adapters.astype(F32) * here)
        return (col_adapter.astype(F32) == a).astype(BF16)

    def picks_at(ahead, core):
        row = 2 * ((x + ahead) % 4) + core
        return picks(lax.dynamic_index_in_dim(ids_all, row, 0, keepdims=False))

    pick = jnp.stack([jnp.tile(picks(ids_all[k]), 3) for k in range(8)])
    pick_all = jnp.concatenate([pick, jnp.zeros((8, 384), BF16)], axis=0)
    pick = [lax.dynamic_slice_in_dim(pick, 2 * x + core, 1) for core in (c, 1 - c)]
    pick = jnp.concatenate([*pick, jnp.zeros((14, 384), BF16)], axis=0)
    pick_f = pick.astype(F32)

    send, normed_attn, small_qkv, gain_attn, gain_mlp = call(
        qkv_kernel,
        [
            shape(16, TOK, 256, dtype=BF16),
            shape(TOK, D, dtype=BF16),
            shape(256, 384, dtype=BF16),
            shape(1, D),
            shape(1, D),
        ],
        [place, x_plane, heads, pick_all, cq, sq, ckv, skv],
        deps=[plane],
        scratch=[
            pltpu.VMEM((1024, D), BF16),
            pltpu.VMEM((1024, 384), BF16),
            pltpu.VMEM((D, 128), F32),
        ],
        specs=[SMEM] + [None] * 7,
        flops=2 * 1024 * D * 768,
        vmem=40,
    )
    mlp_set = lax.all_gather(gate(plane, o_mine, send), NATURAL + ("c",), axis=0, tiled=True)
    z = a2a(a2a(send, "x"), BLOCKS).reshape(GTOK, 256)
    cot = [cot_own, *from_x(gate(cot_own, o_set[1]))]
    cot = jnp.concatenate([cot[1], cot[2], cot[0], cot[3]])

    t2 = jnp.concatenate(
        [
            q_w.reshape(16, 2, 1024).transpose(1, 0, 2),
            kv_w.reshape(16, 2, 512).transpose(1, 0, 2),
            jnp.concatenate(
                [qo.reshape(2, 8, 128), kvo.reshape(2, 4, 128), jnp.zeros((2, 4, 128), BF16)], axis=1
            ),
        ],
        axis=2,
    )
    t2 = chip_rows(t2)
    rel = jnp.stack([t2] + [along_x(t2, k) for k in (1, 2, 3)])
    rel = [lax.dynamic_index_in_dim(rel, (x - k) % 4, 0, keepdims=False) for k in range(4)]
    t2 = jnp.concatenate(rel)

    attended, stat = call(
        attend_kernel,
        [shape(GTOK, 128, dtype=BF16), shape(8, 512)],
        [z],
        deps=o_set[1:3],
        flops=2 * 2 * 2 * 30 * CLEN * CLEN * HDIM * 4,
        vmem=20,
    )
    mine = a2a(attended.reshape(16, TOK, 128), BLOCKS)
    theirs = other_core(mine)
    part, their_part, small_o, attended, o_whole, out_out = call(
        project_kernel,
        [
            shape(TOK, 1024),
            shape(TOK, 1024),
            shape(256, 128, dtype=BF16),
            shape(TOK, D, dtype=BF16),
            shape(D, 1280, dtype=BF16),
            shape(128, D, dtype=BF16),
        ],
        [place, mine, theirs, *o_set, pick],
        scratch=[pltpu.VMEM((2, 256, 1024), BF16), pltpu.VMEM((D, 128), F32)],
        specs=[SMEM] + [None] * 7,
        flops=2 * 256 * D * 1024,
        vmem=24,
    )
    w_spec = block(D, 1536, 0)
    o_spec = block(D, 1024, 0)
    oa_spec = block(D, 128, 8)

    device = jnp.arange(128)
    device_segment = segment_of(((device >> 5) & 1) * 8 + (device >> 6) * 4 + ((device >> 3) & 3))
    device_segment = (device_segment[:, None] == jnp.arange(5)).astype(F32)
    device_ids = jnp.broadcast_to(ids_all[None], (16, 8, 5)).reshape(128, 5)
    device_adapter = jnp.sum(device_ids * device_segment, axis=1)
    natural = device_adapter.astype(jnp.int32)
    device_slot = (natural >> 1 & 1) * 4 + (natural >> 2) * 2 + (natural & 1)
    source_slot = lax.dynamic_slice_in_dim(
        device_slot.reshape(16, 8).T.reshape(128), (2 * x + c) * 16, 16
    )
    lane = jnp.arange(384)
    fold_to = jnp.where(lane < 256, lane // 128, 2) * RANK + lane % RANK
    fold = (fold_to[:, None] == jnp.arange(128)[None, :]).astype(BF16)

    gu_out, down_out = call(
        unpack_kernel,
        [shape(128, 4096, dtype=BF16), shape(128, D, dtype=BF16)],
        [mlp_set[:, 6528:]],
        scratch=[pltpu.VMEM((D, 128), F32)],
        vmem=12,
    )

    hidden, normed_mlp = call(
        hidden_kernel,
        [shape(TOK, D), shape(TOK, D, dtype=BF16)],
        [place, x_own, part, other_core(their_part), gain_mlp],
        deps=[cot],
        specs=[SMEM] + [None] * 4,
        vmem=10,
    )

    pick4 = jnp.concatenate(
        [jnp.broadcast_to(picks_at(ahead, c), (TOK, 128)) for ahead in (3, 1, 0, 2)]
    )
    dm, turned = call(
        turn_kernel, [shape(512, D, dtype=BF16), shape(D, 512, dtype=BF16)], [cot]
    )
    n1, n3 = along_x(normed_mlp, 1), along_x(normed_mlp, 3)
    d_act, d_small_down = tiled_call(
        d_act_kernel,
        [shape(512, 2048), shape(512, 128, dtype=BF16)],
        [dm, turned, down_out, mlp_set, pick4, mlp_set],
        [
            whole_spec(512, D),
            whole_spec(D, 512),
            whole_spec(128, D),
            pl.BlockSpec((512, 128), lambda i: (i, 50)),
            whole_spec(512, 128),
            pl.BlockSpec((512, 2048), lambda i: (i, 2)),
        ],
        [pl.BlockSpec((512, 512), lambda i: (0, i)), whole_spec(512, 128)],
        flops=2 * 512 * 2048 * D,
        vmem=52,
    )

    half_one, half_three = call(
        halves_kernel,
        [shape(TOK // 2, D, dtype=BF16)] * 2,
        [n1, n3],
        deps=[d_act],
        vmem=6,
    )
    n2 = jnp.concatenate([along_x(half_one, 1), along_x(half_three, 3)])
    t2 = lax.all_gather(gate(t2, normed_mlp), NATURAL, axis=0, tiled=True)

    def feed(part, one, two, g_gate, g_up):
        lines = pl.BlockSpec((16, 4, 8, 128), lambda i: (0, i, 0, 0))
        return tiled_call(
            feed_kernel,
            [
                shape(256, 2048, dtype=BF16),
                shape(TOK, D + 384, dtype=BF16),
                shape(TOK, D + 384, dtype=BF16),
                shape(16, 16, 8, 128),
                shape(16, 16, 8, 128),
            ],
            [one, two, d_act, pick4, mlp_set, mlp_set, gu_out, gu_out, mlp_set, mlp_set, g_gate, g_up],
            [
                once(TOK, D),
                once(TOK, D),
                pl.BlockSpec((256, 512), lambda i: (part, i)),
                pl.BlockSpec((256, 128), lambda i: (part, 0)),
                pl.BlockSpec((D, 512), lambda i: (0, i)),
                pl.BlockSpec((D, 512), lambda i: (0, i + 4)),
                pl.BlockSpec((128, 512), lambda i: (0, i)),
                pl.BlockSpec((128, 512), lambda i: (0, i + 4)),
                block(D, 256, 24),
                pl.BlockSpec((512, 128), lambda i: (i, 50)),
                lines,
                lines,
            ],
            [pl.BlockSpec((256, 512), lambda i: (0, i))]
            + [whole_spec(TOK, D + 384)] * 2
            + [lines] * 2,
            [pltpu.VMEM((D + 384, 256), F32), pltpu.VMEM((256, 256), BF16), pltpu.VMEM((256, 256), BF16), pltpu.VMEM((256, D), BF16)],
            flops=2 * 256 * 4096 * D * 2,
            vmem=52,
        )

    none = jnp.zeros((16, 16, 8, 128), F32)
    act_a, back_1, back_3, g_gate, g_up = feed(0, n1, n3, none, none)
    act_b, back_b, back_2, g_gate, g_up = feed(1, normed_mlp, n2, g_gate, g_up)
    back = [along_x(back_1, 3), along_x(back_3, 1), back_b, along_x(back_2, 2)]

    gu_lines = 2.0 * jnp.concatenate([g_gate, g_up], axis=1).reshape(16, 256, 128)
    gu_lines = a2a(gu_lines.astype(BF16), NATURAL)
    *down, g_down_in = tiled_call(
        down_kernel,
        [shape(TOK, D, dtype=BF16)] * 4 + [shape(2048, 128, dtype=BF16)],
        [act_a, act_b, d_small_down, mlp_set],
        [
            pl.BlockSpec((256, 512), lambda i: (0, i)),
            pl.BlockSpec((256, 512), lambda i: (0, i)),
            once(512, 128),
            pl.BlockSpec((512, D), lambda i: (i, 2)),
        ],
        [whole_spec(TOK, D)] * 4 + [pl.BlockSpec((512, 128), lambda i: (i, 0))],
        [pltpu.VMEM((512, D), F32)],
        flops=2 * 512 * 2048 * D,
        deps=[back_b, back[0], back[1]],
        vmem=52,
    )
    d_hidden, d_attn, d_small_gu, small_down = call(
        d_hidden_kernel,
        [
            shape(TOK, D),
            shape(TOK, D, dtype=BF16),
            shape(TOK, 256, dtype=BF16),
            shape(TOK, 128, dtype=BF16),
        ],
        [hidden, cot_own, gain_mlp, *back, mlp_set, pick_f],
        deps=[down[0], gu_lines],
        specs=[None] * 7 + [block(D, 256, 24), None],
        vmem=52,
    )

    mine, theirs, d_small_o, halves = call(
        project_back_kernel,
        [
            shape(256, 1024),
            shape(256, 1024, dtype=BF16),
            shape(256, 128, dtype=BF16),
            shape(256, 1024, dtype=BF16),
        ],
        [place, d_attn, other_core(d_attn), o_whole, o_whole, out_out, pick_f],
        specs=[SMEM, None, None, o_spec, oa_spec, None, None],
        flops=2 * 256 * D * 1024,
        vmem=20,
    )
    (send,) = call(
        pack_kernel, [shape(16, TOK, 128, dtype=BF16)], [mine, other_core(theirs)], vmem=6
    )

    down = [
        along_x(down[0], 3),
        along_x(down[1], 1),
        down[2],
        along_x(down[3], 2),
    ]
    d_out = a2a(send, BLOCKS).reshape(GTOK, 128)
    (early,) = call(
        early_grads_kernel,
        [shape(16, 384, 128, dtype=BF16)],
        [
            g_down_in,
            d_small_gu,
            normed_mlp,
            small_down,
            cot_own,
            d_small_o,
            attended,
            small_o,
            halves,
            fold,
        ],
        scratch=[pltpu.VMEM((16, 384, 128), F32)],
        deps=[d_out],
        vmem=28,
    )
    early = a2a(early, NATURAL)
    q_out, k_out, v_out = call(
        unpack_qkv_kernel,
        [shape(128, 1024, dtype=BF16), shape(128, 512, dtype=BF16), shape(128, 512, dtype=BF16)],
        [t2[:, 1536:]],
        scratch=[pltpu.VMEM((D, 128), F32)],
        vmem=8,
    )
    (dz,) = call(
        attend_back_kernel,
        [shape(GTOK, 256, dtype=BF16)],
        [z, d_out, stat],
        deps=[q_out],
        scratch=[pltpu.VMEM((GTOK, HDIM), F32), pltpu.VMEM((GTOK, HDIM), F32)],
        flops=5 * 2 * 2 * 30 * CLEN * CLEN * HDIM * 4,
        vmem=24,
    )
    parts = a2a(dz.reshape(16, TOK, 256), BLOCKS)
    plane, g_down_in = call(
        sums_kernel,
        [shape(8, 120, 128), shape(128, 128)],
        [source_slot, gu_lines, early],
        deps=[dz],
        scratch=[pltpu.VMEM((512, 128), F32), pltpu.VMEM((256, 128), F32)],
        specs=[SMEM, None, None],
        vmem=14,
    )
    def in_chip(v):
        v = v.reshape(4, 2, *v.shape[1:])

        def to_chip(k):
            return lax.dynamic_index_in_dim(v, (x + k) % 4, 0, keepdims=False)

        by_chip = jnp.stack([to_chip(0)] + [along_x(to_chip(k), k) for k in (1, 2, 3)])
        keep = lax.dynamic_index_in_dim(by_chip, c, 1, keepdims=False)
        return keep, other_core(lax.dynamic_index_in_dim(by_chip, 1 - c, 1, keepdims=False))

    keep, take = in_chip(plane)
    (output,) = call(
        output_kernel,
        [shape(TOK, D, dtype=BF16)],
        [hidden, *down, down_out, small_down],
        deps=[take],
        vmem=12,
    )
    output = swap_mid(output)
    d_joint, mine_small, their_small = call(
        qkv_back_kernel,
        [shape(256, 1536, dtype=BF16), shape(TOK, 384), shape(TOK, 384, dtype=BF16)],
        [parts, q_out, k_out, v_out, cq, sq, ckv, skv],
        deps=[take],
        vmem=12,
    )
    d_small_qkv, late = call(
        late_grads_kernel,
        [shape(TOK, 384, dtype=BF16), shape(D, 256, dtype=BF16)],
        [mine_small, other_core(their_small), pick_f, normed_attn, small_qkv, d_joint, fold],
        scratch=[pltpu.VMEM((D, 128), F32)],
        vmem=14,
    )
    mine, theirs = call(
        d_normed_kernel,
        [shape(TOK, D), shape(TOK, D, dtype=BF16)],
        [d_joint, t2],
        deps=[late],
        specs=[None, w_spec],
        flops=2 * 256 * D * 1536,
        vmem=20,
    )
    late = a2a(late.reshape(128, 16, 256), NATURAL + PLANE)
    (input_grad,) = call(
        last_kernel,
        [shape(TOK, D, dtype=BF16)],
        [x_own, d_hidden, gain_attn, mine, other_core(theirs), d_small_qkv, heads],
        specs=[None] * 6 + [block(D, 384, 1)],
        vmem=14,
    )
    input_grad = swap_mid(input_grad)

    late_first, late_second = call(
        late_sums_kernel,
        [shape(8, 16, 128), shape(2, 16, 128)],
        [device_slot, late],
        specs=[SMEM, None],
        vmem=8,
    )
    both = keep + take
    gu = both[:, :32]
    gu = [lax.dynamic_index_in_dim(gu, (x - k) % 4, 0, keepdims=False) for k in range(4)]
    gu = jnp.stack(gu).reshape(4, 2, 2, 2, 4, 128).transpose(1, 3, 2, 4, 0, 5)
    grad_gu_out = gu.reshape(1, 2 * UNITS)
    half = g_down_in.reshape(2, 64, 128)
    to_other = lax.dynamic_index_in_dim(half, 1 - c, 0, keepdims=False)
    grad_down_in = lax.dynamic_index_in_dim(half, c, 0, keepdims=False)
    grad_down_in = swap_mid(grad_down_in + other_core(to_other))
    total = jnp.sum(both[:, 32:112], axis=0)
    first = total[:64].reshape(4, 16, 2, 4, RANK).transpose(1, 3, 0, 2, 4).reshape(16, 4, 128)
    grad_gu_in = swap_mid(first[:, :2]).reshape(16, 256)
    grad_out_in = swap_mid(first[:, 2])
    grad_down_out = swap_mid(total[64:80].reshape(1, D))
    keep, take = jnp.sum(keep[:, 112:], axis=0), jnp.sum(take[:, 112:], axis=0)
    halves = jnp.where(c == 0, jnp.stack([keep, take]), jnp.stack([take, keep]))
    grad_out_out = swap_mid(halves.reshape(1, D))
    first = late_first[:, :, :48].reshape(8, 16, 3, RANK).transpose(1, 2, 0, 3)
    grad_qkv_in = swap_mid(first.reshape(16, 3, 128)).reshape(16, 384)
    grad_q_out = swap_mid(late_second[:, :8].reshape(1, D))
    kv = late_second[:, 8:12].reshape(2, 4, 2, HDIM).transpose(2, 0, 1, 3).reshape(2, 512)
    grad_kv_out = swap_mid(kv).reshape(1, 1024)

    return (
        output[None],
        input_grad[None],
        grad_qkv_in,
        grad_q_out,
        grad_kv_out,
        grad_out_in,
        grad_out_out,
        grad_gu_in,
        grad_gu_out,
        grad_down_in,
        grad_down_out,
    )


def solution(mesh):
    fine = Mesh(mesh.devices.reshape(2, 2, 4, 4, 2), AXES)
    tok = P(PLANE, BLOCKS, None)
    flat = P(AXES)
    rows = P(AXES, None)
    return jax.shard_map(
        local,
        mesh=fine,
        in_specs=(tok, P(PLANE, None), flat, flat) + (rows,) * 13 + (tok,),
        out_specs=(tok, tok) + (rows,) * 9,
        check_vma=False,
    )
```
